256 devices in a mesh: tx: 8 (over z_hi, y), rx: 32 (over x, z_lo, core).
Axes of the slice: x: 4, y: 4, z: 8 (z_hi: 2, z_lo: 4; z = z_hi * 4 + z_lo), core: 2. Of those that a mesh axis runs over, the one named last changes fastest.
Arguments:
- slowness: bfloat16 [32], replicated, may hold values from -4 to 4
- tx_paths: bfloat16 [64, 32, 4096], P('tx', None, 'rx'), may hold values from 0 to 0.25
- rx_paths: bfloat16 [1024, 32, 4096], P('rx'), may hold values from 0 to 0.25
- traces: bfloat16 [64, 1024, 512], P('tx', 'rx'), may hold values from -6 to 6
- tap_start: int32 [64, 1024, 32], P('tx', 'rx'), may hold values from 0 to 504
- pixel_order: int32 [4096], replicated, may hold values from 0 to 4095, each once
- patch_cotangent: float32 [16], replicated, may hold values from 30 to 300
Outputs:
- slowness_grad: float32 [32], replicated
The draws below stay inside these ranges and needn't reach their ends.
Inputs may be any that keep to these rules, and one draw needn't show every extreme that they name: `pixel_order`: each pixel rank occurs once, so every patch holds 256 pixels.
All inputs are finite; a program needn't handle non-finite values.
Results may differ from the reference program's by a relative error of at most 0.00085.
Values may be sent and summed in bfloat16 or wider, within the bound.
No kernel may reach another device: no remote copies, remote signals or barrier semaphores. Data moves between devices by JAX's collectives and lax.ppermute only.
A program may use at most 64 MiB of HBM per device.

```python
import math
import jax
import jax.numpy as jnp
from jax import lax

G = 32
P_SIZE = 4096
K = 512
W = 8
PB = 128
PP = 256
TXS = 64
RXS = 1024
NBLK = 32
NPATCH = 16


def touch_ends(entries, stream_key, smallest, top_value):
    longest = entries.shape.index(max(entries.shape))
    spots = []
    for shift in (0, 1):
        where = [jax.random.randint(jax.random.fold_in(stream_key, axis), (), 0, length) for axis, length in enumerate(entries.shape)]
        where[longest] = (where[longest] + shift) % entries.shape[longest]
        spots.append(tuple(where))
    return entries.at[spots[0]].set(smallest).at[spots[1]].set(top_value)


def levels(key, shape, cuts, low, largest):
    gain, own = 1.0, jax.random.fold_in(key, 6)
    for dim, blocks in cuts:
        draws = jnp.exp(jax.random.uniform(jax.random.fold_in(own, dim), (blocks,), jnp.float32, low / len(cuts), largest / len(cuts)))
        gain = gain * jnp.repeat(draws, shape[dim] // blocks).reshape([-1 if axis == dim else 1 for axis in range(len(shape))])
    return gain


def gaussian(key, shape, spread, bound, pieces=(), kind=jnp.bfloat16):
    drawn = jax.random.normal(key, shape, jnp.float32) * spread
    if len(pieces) > 0:
        drawn = levels(key, shape, pieces, -0.22, 0.18) * drawn
    return jnp.clip(drawn, min=-bound, max=bound).astype(kind)


def setup_inputs(seed: int = 0) -> dict:
    key_list = jax.random.split(jax.random.key(seed), 8)
    return {
        "slowness": gaussian(key_list[0], (G,), 1.0, 4.0),
        "tx_paths": jnp.clip(0.25 * jax.random.uniform(key_list[1], (TXS, G, P_SIZE), jnp.float32) ** levels(key_list[1], (TXS, G, P_SIZE), ((0, 8), (2, 32)), -0.2, 0.2), 0.0, 0.25).astype(jnp.bfloat16),
        "rx_paths": jnp.clip(0.25 * jax.random.uniform(key_list[2], (RXS, G, P_SIZE), jnp.float32) ** levels(key_list[2], (RXS, G, P_SIZE), ((0, 32),), -0.2, 0.2), 0.0, 0.25).astype(jnp.bfloat16),
        "traces": gaussian(key_list[3], (TXS, RXS, K), 1.0, 6.0, ((0, 8), (1, 32))),
        "tap_start": touch_ends(jax.random.randint(key_list[4], (TXS, RXS, NBLK), 0, K - W + 1), jax.random.fold_in(key_list[4], 1), 0, K - W).astype(jnp.int32),
        "pixel_order": jax.random.permutation(key_list[5], P_SIZE).astype(jnp.int32),
        "patch_cotangent": jnp.clip(jnp.exp(jax.random.uniform(key_list[6], (NPATCH,), jnp.float32, math.log(30.0), math.log(300.0))), 30.0, 300.0),
    }


EPS = 1e-6


def windows_of(traces, tap_start):
    positions = tap_start[..., None] + jnp.arange(W, dtype=jnp.int32)
    flat = positions.reshape(TXS, RXS, NBLK * W).astype(jnp.int32)
    picked = jnp.take_along_axis(traces, flat, axis=2)
    return picked.astype(jnp.float32).reshape(TXS, RXS, NBLK, W)


def focus_one(tx_row, window_row, rx_delay):
    tau = (W - 1) / 2.0 + tx_row[None, :] + rx_delay
    tau = tau.reshape(RXS, NBLK, PB)
    focused = jnp.zeros((RXS, NBLK, PB), jnp.float32)
    slope = jnp.zeros((RXS, NBLK, PB), jnp.float32)
    for position in range(W):
        offset = tau - position
        kernel = jnp.exp(-0.5 * offset * offset)
        sample = window_row[:, :, position][:, :, None]
        focused = focused + kernel * sample
        slope = slope - offset * kernel * sample
    return focused, slope


def reference(slowness, tx_paths, rx_paths, traces, tap_start, pixel_order, patch_cotangent):
    hi = lax.Precision.HIGHEST
    slow_cells = slowness.astype(jnp.float32)
    tx_delay = jnp.einsum('tgp,g->tp', tx_paths.astype(jnp.float32), slow_cells, precision=hi)
    rx_delay = jnp.einsum('rgp,g->rp', rx_paths.astype(jnp.float32), slow_cells, precision=hi)
    window = windows_of(traces, tap_start)

    def beam_row(pair):
        focused, slope = focus_one(pair[0], pair[1], rx_delay)
        return focused.sum(0).reshape(P_SIZE)

    beam = lax.map(beam_row, (tx_delay, window))
    coherent = beam.sum(0)
    power = (beam * beam).sum(0)
    patch_ids = (pixel_order // PP).astype(jnp.int32)
    table = (patch_ids[None, :] == jnp.arange(NPATCH, dtype=jnp.int32)[:, None]).astype(jnp.float32)
    numer = jnp.dot(table, coherent * coherent, precision=hi)
    denom = TXS * jnp.dot(table, power, precision=hi)
    scale_num = jnp.dot(patch_cotangent / (numer + EPS), table, precision=hi)
    scale_den = jnp.dot(patch_cotangent * TXS / (denom + EPS), table, precision=hi)
    beam_grad = -2.0 * (coherent * scale_num)[None, :] + 2.0 * beam * scale_den[None, :]

    def step(carry, triple):
        focused, slope = focus_one(triple[0], triple[1], rx_delay)
        delay_grad = triple[2].reshape(1, NBLK, PB) * slope
        return carry + delay_grad.reshape(RXS, P_SIZE), delay_grad.sum(0).reshape(P_SIZE)

    rx_sum, tx_sum = lax.scan(step, jnp.zeros((RXS, P_SIZE), jnp.float32), (tx_delay, window, beam_grad))
    grad_tx = jnp.einsum('tgp,tp->g', tx_paths.astype(jnp.float32), tx_sum, precision=hi)
    grad_rx = jnp.einsum('rgp,rp->g', rx_paths.astype(jnp.float32), rx_sum, precision=hi)
    return grad_tx + grad_rx
```

```python
import math

import jax
import jax.numpy as jnp
from jax import lax
from jax.experimental import pallas as pl
from jax.experimental.pallas import tpu as pltpu
from jax.sharding import PartitionSpec as P

W = 8
PB = 128
PP = 256
EPS = 1e-06
LN2 = math.log(2.0)
HALF_LOG2E = 0.5 / LN2
F32 = jnp.float32
VMEM_LIMIT = 48 * 1024 * 1024


def block_diagonal(s_row, rows, cells):
    wide = jnp.concatenate([s_row] * rows, axis=1)
    shape = (rows, rows * cells)
    owner = lax.broadcasted_iota(jnp.int32, shape, 1) // cells
    mine = owner == lax.broadcasted_iota(jnp.int32, shape, 0)
    return jnp.where(mine, jnp.broadcast_to(wide, shape), 0.0).astype(jnp.bfloat16)


def tx_delay_kernel(s_ref, path_ref, out_ref):
    rows, cells, width = path_ref.shape
    left = block_diagonal(s_ref[...].astype(F32), rows, cells)
    delay = jnp.dot(
        left, path_ref[...].reshape(rows * cells, width), preferred_element_type=F32
    )
    out_ref[...] = jnp.broadcast_to((delay * HALF_LOG2E)[None], out_ref.shape)


def prepare_kernel(s_ref, path_ref, trace_ref, start_ref, delay_ref, win_ref):
    rows, cells, width = path_ref.shape
    left = block_diagonal(s_ref[...].astype(F32), 8, cells)
    for first in range(0, rows, 8):
        paths = path_ref[pl.ds(first, 8)].reshape(8 * cells, width)
        delay = jnp.dot(left, paths, preferred_element_type=F32)
        delay_ref[pl.ds(first, 8), :] = delay * HALF_LOG2E
    samples = trace_ref[0].astype(F32)
    starts = start_ref[0]
    blocks = starts.shape[1]
    per = 128 // blocks
    starts = jnp.concatenate([starts] * per, axis=1)
    lane = lax.broadcasted_iota(jnp.int32, starts.shape, 1)
    for half in range(W // per):
        tap = lane // blocks + half * per
        index = starts + tap
        low = index & 127
        high = index >> 7
        picked = None
        for part in range(samples.shape[1] // 128):
            source = samples[:, part * 128 : (part + 1) * 128]
            got = jnp.take_along_axis(source, low, axis=1, mode="promise_in_bounds")
            picked = got if picked is None else jnp.where(high == part, got, picked)
        off = tap.astype(F32) - (W - 1) / 2.0
        win_ref[0, :, half * 128 : (half + 1) * 128] = picked * jnp.exp(-0.5 * off * off)


def focus_kernel(tx_ref, rx_ref, win_ref, slope_ref, sum_ref):
    t = pl.program_id(0)
    blocks = tx_ref.shape[0]
    rows = rx_ref.shape[0]
    per = 128 // blocks
    limit = 9.25 / LN2

    def point(k, first):
        def tap(j):
            lane = (j // per) * 128 + (j % per) * blocks + k
            return jnp.broadcast_to(win_ref[0, first : first + 8, lane : lane + 1], (8, PB))

        h = tx_ref[k, pl.ds(t, 1), :] + rx_ref[first : first + 8, k * PB : (k + 1) * PB]
        h = jnp.minimum(jnp.maximum(h, -limit), limit)
        m = h * (-LN2)
        s = jnp.exp2(h)
        si = jnp.exp2(-h)
        gauss = jnp.exp2(m * h)
        u = s * s
        v = si * si

        def horner(z, c3, c2, c1, c0):
            p1 = c3 * z + c2
            p2 = p1 * z + c1
            d2 = c3 * z + p1
            return p2 * z + c0, d2 * z + p2

        up, dup = horner(u, tap(7), tap(6), tap(5), tap(4))
        down, ddown = horner(v, tap(0), tap(1), tap(2), tap(3))
        x = s * up
        y = si * down
        both = x + y
        change = (x - y) * 0.5 + ((s * u) * dup - (si * v) * ddown)
        focused = gauss * (gauss * both)
        slope = gauss * (gauss * (change + (m + m) * both))
        return focused, slope

    for k in range(blocks):
        total_f = None
        total_s = None
        for first in range(0, rows, 8):
            focused, slope = point(k, first)
            slope_ref[0, first : first + 8, k * PB : (k + 1) * PB] = slope
            total_f = focused if total_f is None else total_f + focused
            total_s = slope if total_s is None else total_s + slope
        count = pl.num_programs(0)
        sum_ref[k, pl.ds(t, 1), :] = jnp.sum(total_f, axis=0, keepdims=True)
        sum_ref[k, pl.ds(count + t, 1), :] = jnp.sum(total_s, axis=0, keepdims=True)


def gather_sum_kernel(part_ref, red_ref, rep_ref):
    total = part_ref[0]
    for i in range(1, part_ref.shape[0]):
        total = total + part_ref[i]
    red_ref[...] = total
    beam = total[0 : total.shape[0] // 2]
    coherent = jnp.sum(beam, axis=0, keepdims=True)
    power = jnp.sum(beam * beam, axis=0, keepdims=True)
    pair = jnp.concatenate([coherent, power], axis=0)
    rep_ref[...] = jnp.broadcast_to(pair[None], rep_ref.shape)


def spread_kernel(pair_ref, red_ref, out_ref):
    pair = pair_ref[0]
    for i in range(1, pair_ref.shape[0]):
        pair = pair + pair_ref[i]
    count = red_ref.shape[0] // 2
    out_ref[:, 0:count, :] = jnp.broadcast_to(
        red_ref[0:count, :][None], (out_ref.shape[0], count, PB)
    )
    out_ref[:, count : count + 2, :] = jnp.broadcast_to(
        pair[None], (out_ref.shape[0], 2, PB)
    )


def gradient_kernel(
    total_tx,
    me_ref,
    cot_ref,
    all_ref,
    ids_ref,
    red_ref,
    tx_path_ref,
    slope_ref,
    path_ref,
    out_ref,
    bg_ref,
    acc_ref,
):
    step = pl.program_id(0)
    count, rows, width = slope_ref.shape
    blocks = all_ref.shape[0]
    cells = path_ref.shape[1]
    patches = cot_ref.shape[0]

    @pl.when(step == 0)
    def _():
        ids = ids_ref[...] // PP
        coherent = all_ref[:, count, :]
        power = all_ref[:, count + 1, :]
        square = coherent * coherent
        scale_n = jnp.zeros_like(square)
        scale_d = jnp.zeros_like(square)
        for q in range(patches):
            inside = ids == q
            numer = jnp.sum(jnp.where(inside, square, 0.0), keepdims=True)
            denom = total_tx * jnp.sum(jnp.where(inside, power, 0.0), keepdims=True)
            cot = jnp.full((1, 1), cot_ref[q], F32)
            value_n = -2.0 * (cot / (numer + EPS))
            value_d = 2.0 * (cot * total_tx / (denom + EPS))
            scale_n = jnp.where(inside, value_n, scale_n)
            scale_d = jnp.where(inside, value_d, scale_d)
        common = coherent * scale_n
        for k in range(blocks):
            bg_ref[k] = common[k : k + 1, :] + all_ref[k, 0:count, :] * scale_d[k : k + 1, :]
        own = bg_ref[me_ref[0]] * red_ref[count : 2 * count, :]
        acc = jnp.zeros((cells, PB), F32)
        for t in range(count):
            acc = acc + tx_path_ref[t].astype(F32) * own[t : t + 1, :]
        acc_ref[...] = acc

    acc = [acc_ref[...], jnp.zeros((cells, PB), F32)]
    for kk in range(width // PB):
        lanes = slice(kk * PB, (kk + 1) * PB)
        bg = bg_ref[step * (width // PB) + kk]
        for first in range(0, rows, 8):
            grad = None
            for t in range(count):
                term = bg[t : t + 1, :] * slope_ref[t, first : first + 8, lanes]
                grad = term if grad is None else grad + term
            for r in range(8):
                paths = path_ref[first + r, :, lanes].astype(F32)
                acc[r % 2] = acc[r % 2] + paths * grad[r : r + 1, :]
    acc = acc[0] + acc[1]
    acc_ref[...] = acc

    @pl.when(step == pl.num_programs(0) - 1)
    def _():
        ones = jnp.ones((8, PB), F32)
        row = lax.dot_general(
            ones,
            acc,
            (((1,), (1,)), ((), ())),
            precision=lax.Precision.HIGHEST,
            preferred_element_type=F32,
        )
        row = jnp.concatenate([row] * (PB // cells), axis=1)
        out_ref[...] = jnp.broadcast_to(row[0:1, :], out_ref.shape)


def params(**more):
    return pltpu.CompilerParams(vmem_limit_bytes=VMEM_LIMIT, **more)


def whole(shape):
    return pl.BlockSpec(shape, lambda *_: (0,) * len(shape))


def on_device(slowness, tx_paths, rx_paths, traces, tap_start, pixel_order, patch_cotangent):
    tx_count, cells, own_pixels = tx_paths.shape
    rx_count, _, pixels = rx_paths.shape
    blocks = pixels // PB
    samples = traces.shape[2]
    tx_size = lax.axis_size("tx")
    rx_size = lax.axis_size("rx")
    total_tx = tx_count * tx_size
    s_row = slowness.reshape(1, cells)
    chunk = pixels // tx_count

    delay = pl.pallas_call(
        tx_delay_kernel,
        out_shape=jax.ShapeDtypeStruct((rx_size, tx_count, own_pixels), F32),
        compiler_params=params(),
        name="tx_delay",
    )(s_row, tx_paths)
    rx_delay, window = pl.pallas_call(
        prepare_kernel,
        grid=(tx_count,),
        in_specs=[
            whole((1, cells)),
            pl.BlockSpec((rx_count, cells, chunk), lambda i: (0, 0, i)),
            pl.BlockSpec((1, rx_count, samples), lambda i: (i, 0, 0)),
            pl.BlockSpec((1, rx_count, blocks), lambda i: (i, 0, 0)),
        ],
        out_specs=[
            pl.BlockSpec((rx_count, chunk), lambda i: (0, i)),
            pl.BlockSpec((1, rx_count, W * blocks), lambda i: (i, 0, 0)),
        ],
        out_shape=[
            jax.ShapeDtypeStruct((rx_count, pixels), F32),
            jax.ShapeDtypeStruct((tx_count, rx_count, W * blocks), F32),
        ],
        compiler_params=params(),
        name="prepare",
    )(s_row, rx_paths, traces, tap_start)
    tx_delay = lax.all_to_all(delay, "rx", 0, 0)
    slope, part = pl.pallas_call(
        focus_kernel,
        grid=(tx_count,),
        in_specs=[
            whole((blocks, tx_count, PB)),
            whole((rx_count, pixels)),
            pl.BlockSpec((1, rx_count, W * blocks), lambda i: (i, 0, 0)),
        ],
        out_specs=[
            pl.BlockSpec((1, rx_count, pixels), lambda i: (i, 0, 0)),
            whole((blocks, 2 * tx_count, PB)),
        ],
        out_shape=[
            jax.ShapeDtypeStruct((tx_count, rx_count, pixels), F32),
            jax.ShapeDtypeStruct((blocks, 2 * tx_count, PB), F32),
        ],
        compiler_params=params(),
        name="focus",
    )(tx_delay, rx_delay, window)
    part = lax.all_to_all(part, "rx", 0, 0)
    red, pair = pl.pallas_call(
        gather_sum_kernel,
        out_shape=[
            jax.ShapeDtypeStruct((2 * tx_count, PB), F32),
            jax.ShapeDtypeStruct((tx_size, 2, PB), F32),
        ],
        compiler_params=params(),
        name="sum_receivers",
    )(part)
    pair = lax.all_to_all(pair, "tx", 0, 0)
    spread = pl.pallas_call(
        spread_kernel,
        out_shape=jax.ShapeDtypeStruct((rx_size, tx_count + 2, PB), F32),
        compiler_params=params(),
        name="sum_transmits",
    )(pair, red)
    every = lax.all_to_all(spread, "rx", 0, 0)
    me = lax.axis_index("rx").astype(jnp.int32).reshape(1)
    smem = pl.BlockSpec(memory_space=pltpu.SMEM)
    share = pl.pallas_call(
        lambda *refs: gradient_kernel(total_tx, *refs),
        grid=(tx_count,),
        in_specs=[
            smem,
            smem,
            whole((blocks, tx_count + 2, PB)),
            whole((blocks, PB)),
            whole((2 * tx_count, PB)),
            whole((tx_count, cells, own_pixels)),
            pl.BlockSpec((tx_count, rx_count, chunk), lambda i: (0, 0, i)),
            pl.BlockSpec((rx_count, cells, chunk), lambda i: (0, 0, i)),
        ],
        out_specs=whole((tx_size * rx_size, PB)),
        out_shape=jax.ShapeDtypeStruct((tx_size * rx_size, PB), F32),
        scratch_shapes=[
            pltpu.VMEM((blocks, tx_count, PB), F32),
            pltpu.VMEM((cells, PB), F32),
        ],
        compiler_params=params(),
        name="gradient",
    )(
        me,
        patch_cotangent,
        every,
        pixel_order.reshape(blocks, PB),
        red,
        tx_paths,
        slope,
        rx_paths,
    )
    share = lax.all_to_all(share, ("tx", "rx"), 0, 0, tiled=True)
    return share.sum(0)[:cells]


def solution(mesh):
    in_specs = (
        P(),
        P("tx", None, "rx"),
        P("rx", None, None),
        P("tx", "rx", None),
        P("tx", "rx", None),
        P(),
        P(),
    )
    out_specs = P()
    return jax.shard_map(
        on_device, mesh=mesh, in_specs=in_specs, out_specs=out_specs, check_vma=False
    )
```

```python
import math

import jax
import jax.numpy as jnp
from jax import lax
from jax.experimental import pallas as pl
from jax.experimental.pallas import tpu as pltpu
from jax.sharding import PartitionSpec as P

W = 8
PB = 128
PP = 256
EPS = 1e-06
LN2 = math.log(2.0)
HALF_LOG2E = 0.5 / LN2
F32 = jnp.float32


def block_diagonal(s_row, rows, cells):
    wide = jnp.concatenate([s_row] * rows, axis=1)
    shape = (rows, rows * cells)
    owner = lax.broadcasted_iota(jnp.int32, shape, 1) // cells
    mine = owner == lax.broadcasted_iota(jnp.int32, shape, 0)
    return jnp.where(mine, jnp.broadcast_to(wide, shape), 0.0).astype(jnp.bfloat16)


def tx_delay_kernel(s_ref, path_ref, out_ref):
    rows, cells, width = path_ref.shape
    left = block_diagonal(s_ref[...].astype(F32), rows, cells)
    delay = jnp.dot(
        left, path_ref[...].reshape(rows * cells, width), preferred_element_type=F32
    )
    out_ref[...] = jnp.broadcast_to((delay * HALF_LOG2E)[None], out_ref.shape)


def prepare_kernel(s_ref, path_ref, trace_ref, start_ref, delay_ref, win_ref, sample_ref, plain_ref):
    step = pl.program_id(0)
    rows, cells, pixels = path_ref.shape
    count = trace_ref.shape[0]
    blocks = start_ref.shape[2]
    per = 128 // blocks

    @pl.when(step == 0)
    def _():
        sample_ref[...] = trace_ref[...].astype(F32)

    left = block_diagonal(s_ref[...].astype(F32), rows, cells)
    delay = jnp.dot(
        left, path_ref[...].reshape(rows * cells, pixels), preferred_element_type=F32
    )
    delay = delay * HALF_LOG2E
    for k in range(blocks):
        plain_ref[:, k, :] = delay[:, k * PB : (k + 1) * PB]
    for r in range(rows):
        delay_ref[r] = jnp.concatenate([plain_ref[r]] * per, axis=0).T

    mine = pl.ds(pl.multiple_of(step * rows, rows), rows)
    shape = (rows, 128)
    group = lax.broadcasted_iota(jnp.int32, shape, 1) // blocks
    for early in range(0, count, per):
        picks = []
        for t in range(early, early + per):
            starts = jnp.concatenate([start_ref[t, mine, :]] * per, axis=1)
            for first in range(0, W, per):
                index = starts + (group + first)
                low = index & 127
                high = index >> 7
                picked = None
                for part in range(sample_ref.shape[2] // 128):
                    source = sample_ref[t, mine, part * 128 : (part + 1) * 128]
                    got = jnp.take_along_axis(source, low, axis=1, mode="promise_in_bounds")
                    picked = got if picked is None else jnp.where(high == part, got, picked)
                picks.append(picked)
        for j in range(W):
            total = None
            for i in range(per):
                rolled = picks[i * (W // per) + j // per]
                shift = ((i - j % per) * blocks) % 128
                if shift:
                    rolled = pltpu.roll(rolled, shift, 1)
                total = rolled if total is None else jnp.where(group == i, rolled, total)
            off = j - (W - 1) / 2.0
            lanes = slice(early * blocks, early * blocks + 128)
            win_ref[:, j, lanes] = total * math.exp(-0.5 * off * off)


def focus_kernel(tx_ref, rx_ref, win_ref, slope_ref, sum_ref, tx_lane_ref, total_f_ref, total_s_ref):
    blocks, count, _ = tx_ref.shape
    rows = rx_ref.shape[0]
    per = 128 // blocks
    limit = 9.25 / LN2
    halves = count // per

    for half in range(halves):
        stack = [tx_ref[:, half * per + i, :] for i in range(per)]
        tx_lane_ref[:, half * 128 : (half + 1) * 128] = jnp.concatenate(stack, axis=0).T
    total_f_ref[...] = jnp.zeros_like(total_f_ref)
    total_s_ref[...] = jnp.zeros_like(total_s_ref)

    def horner(z, c3, c2, c1, c0):
        p1 = c3 * z + c2
        p2 = p1 * z + c1
        d2 = c3 * z + p1
        return p2 * z + c0, d2 * z + p2

    def point(tap, h):
        h = jnp.minimum(jnp.maximum(h, -limit), limit)
        m = h * (-LN2)
        s = jnp.exp2(h)
        si = jnp.exp2(-h)
        gauss = jnp.exp2(m * h)
        u = s * s
        v = si * si
        up, dup = horner(u, tap[7], tap[6], tap[5], tap[4])
        down, ddown = horner(v, tap[0], tap[1], tap[2], tap[3])
        x = s * up
        y = si * down
        both = x + y
        change = (x - y) * 0.5 + ((s * u) * dup - (si * v) * ddown)
        focused = gauss * (gauss * both)
        slope = gauss * (gauss * (change + (m + m) * both))
        return focused, slope

    def receiver(r, carry):
        for half in range(halves):
            lanes = slice(half * 128, (half + 1) * 128)
            tap = [
                jnp.broadcast_to(win_ref[r, j : j + 1, lanes], (8, 128)) for j in range(W)
            ]
            for first in range(0, PB, 8):
                here = slice(first, first + 8)
                h = tx_lane_ref[here, lanes] + rx_ref[r, here, :]
                focused, slope = point(tap, h)
                slope_ref[r, here, lanes] = slope
                total_f_ref[here, lanes] += focused
                total_s_ref[here, lanes] += slope
        return carry

    lax.fori_loop(0, rows, receiver, 0)
    for source, base in ((total_f_ref, 0), (total_s_ref, count)):
        for half in range(halves):
            turned = source[:, half * 128 : (half + 1) * 128].T
            for i in range(per):
                sum_ref[:, base + half * per + i, :] = turned[i * blocks : (i + 1) * blocks]


def gather_sum_kernel(part_ref, red_ref, rep_ref):
    total = part_ref[0]
    for i in range(1, part_ref.shape[0]):
        total = total + part_ref[i]
    red_ref[...] = total
    beam = total[0 : total.shape[0] // 2]
    coherent = jnp.sum(beam, axis=0, keepdims=True)
    power = jnp.sum(beam * beam, axis=0, keepdims=True)
    pair = jnp.concatenate([coherent, power], axis=0)
    rep_ref[...] = jnp.broadcast_to(pair[None], rep_ref.shape)


def spread_kernel(pair_ref, red_ref, out_ref):
    pair = pair_ref[0]
    for i in range(1, pair_ref.shape[0]):
        pair = pair + pair_ref[i]
    count = red_ref.shape[0] // 2
    out_ref[:, 0:count, :] = jnp.broadcast_to(
        red_ref[0:count, :][None], (out_ref.shape[0], count, PB)
    )
    out_ref[:, count : count + 2, :] = jnp.broadcast_to(
        pair[None], (out_ref.shape[0], 2, PB)
    )


def patch_scales(total_tx, cot_ref, ids, coherent, power):
    patches = cot_ref.shape[0]
    square = coherent * coherent
    sums = []
    for field in (square, power):
        rows = [
            jnp.sum(jnp.where(ids == q, field, 0.0), axis=0, keepdims=True)
            for q in range(patches)
        ]
        sums.append(jnp.sum(jnp.concatenate(rows, axis=0), axis=1, keepdims=True))
    numer, power_sum = sums
    denom = total_tx * power_sum
    cot = cot_ref[...]
    value_n = -2.0 * (cot / (numer + EPS))
    value_d = 2.0 * (cot * total_tx / (denom + EPS))
    scale_n = jnp.zeros_like(square)
    scale_d = jnp.zeros_like(square)
    for q in range(patches):
        inside = ids == q
        scale_n = jnp.where(inside, value_n[q : q + 1, :], scale_n)
        scale_d = jnp.where(inside, value_d[q : q + 1, :], scale_d)
    return scale_n, scale_d


def gradient_kernel(
    total_tx,
    me_ref,
    cot_ref,
    all_ref,
    ids_ref,
    red_ref,
    tx_path_ref,
    slope_ref,
    path_ref,
    out_ref,
    bg_ref,
    bg_lane_ref,
    grad_ref,
    acc_ref,
):
    step = pl.program_id(0)
    rows, cells, _ = path_ref.shape
    blocks = all_ref.shape[0]
    count = red_ref.shape[0] // 2
    per = 128 // blocks

    @pl.when(step == 0)
    def _():
        coherent = all_ref[:, count, :]
        power = all_ref[:, count + 1, :]
        scale_n, scale_d = patch_scales(total_tx, cot_ref, ids_ref[...] // PP, coherent, power)
        common = coherent * scale_n
        for t in range(count):
            bg_ref[t] = common + all_ref[:, t, :] * scale_d
        for half in range(count // per):
            stack = [bg_ref[half * per + i] for i in range(per)]
            bg_lane_ref[:, half * 128 : (half + 1) * 128] = jnp.concatenate(stack, axis=0).T
        acc = jnp.zeros((cells, PB), F32)
        for t in range(count):
            own = bg_ref[t, pl.ds(me_ref[0], 1), :] * red_ref[count + t : count + t + 1, :]
            acc = acc + tx_path_ref[t].astype(F32) * own
        acc_ref[...] = acc

    acc = [acc_ref[...], jnp.zeros((cells, PB), F32)]
    for r in range(rows):
        grad = None
        for half in range(count // per):
            lanes = slice(half * 128, (half + 1) * 128)
            term = slope_ref[r, :, lanes] * bg_lane_ref[:, lanes]
            grad = term if grad is None else grad + term
        grad = grad.T
        total = grad[0:blocks]
        for i in range(1, per):
            total = total + grad[i * blocks : (i + 1) * blocks]
        grad_ref[r] = total
        for k in range(blocks):
            paths = path_ref[r, :, k * PB : (k + 1) * PB].astype(F32)
            acc[k % 2] = acc[k % 2] + paths * grad_ref[r, k : k + 1, :]
    acc = acc[0] + acc[1]
    acc_ref[...] = acc

    @pl.when(step == pl.num_programs(0) - 1)
    def _():
        ones = jnp.ones((8, PB), F32)
        row = lax.dot_general(
            ones,
            acc,
            (((1,), (1,)), ((), ())),
            precision=lax.Precision.HIGHEST,
            preferred_element_type=F32,
        )
        row = jnp.concatenate([row] * (PB // cells), axis=1)
        out_ref[...] = jnp.broadcast_to(row[0:1, :], out_ref.shape)


def params(megabytes):
    return pltpu.CompilerParams(vmem_limit_bytes=megabytes * 1024 * 1024)


def whole(shape):
    return pl.BlockSpec(shape, lambda *_: (0,) * len(shape))


def shaped(*shape):
    return jax.ShapeDtypeStruct(shape, F32)


def tx_delays(s_row, tx_paths, rx_size):
    tx_count, _, own_pixels = tx_paths.shape
    return pl.pallas_call(
        tx_delay_kernel,
        out_shape=shaped(rx_size, tx_count, own_pixels),
        compiler_params=params(4),
        name="tx_delay",
    )(s_row, tx_paths)


def prepare(s_row, rx_paths, traces, tap_start):
    rx_count, cells, pixels = rx_paths.shape
    tx_count, _, samples = traces.shape
    blocks = pixels // PB
    rows = 8
    return pl.pallas_call(
        prepare_kernel,
        grid=(rx_count // rows,),
        in_specs=[
            whole((1, cells)),
            pl.BlockSpec((rows, cells, pixels), lambda i: (i, 0, 0)),
            whole((tx_count, rx_count, samples)),
            whole((tx_count, rx_count, blocks)),
        ],
        out_specs=[
            pl.BlockSpec((rows, PB, 128), lambda i: (i, 0, 0)),
            pl.BlockSpec((rows, W, tx_count * blocks), lambda i: (i, 0, 0)),
        ],
        out_shape=[shaped(rx_count, PB, 128), shaped(rx_count, W, tx_count * blocks)],
        scratch_shapes=[
            pltpu.VMEM((tx_count, rx_count, samples), F32),
            pltpu.VMEM((rows, blocks, PB), F32),
        ],
        compiler_params=params(12),
        name="prepare",
    )(s_row, rx_paths, traces, tap_start)


def focus(tx_delay, rx_delay, window):
    blocks, tx_count, _ = tx_delay.shape
    rx_count = rx_delay.shape[0]
    lanes = tx_count * blocks
    return pl.pallas_call(
        focus_kernel,
        out_shape=[shaped(rx_count, PB, lanes), shaped(blocks, 2 * tx_count, PB)],
        scratch_shapes=[pltpu.VMEM((PB, lanes), F32)] * 3,
        compiler_params=params(12),
        name="focus",
    )(tx_delay, rx_delay, window)


def gradient(total_tx, parts, me, patch_cotangent, every, pixel_order, red, tx_paths, slope, rx_paths):
    rx_count, cells, pixels = rx_paths.shape
    blocks = pixels // PB
    tx_count = tx_paths.shape[0]
    lanes = tx_count * blocks
    rows = 4
    return pl.pallas_call(
        lambda *refs: gradient_kernel(total_tx, *refs),
        grid=(rx_count // rows,),
        in_specs=[
            pl.BlockSpec(memory_space=pltpu.SMEM),
            whole((patch_cotangent.shape[0], 1)),
            whole(every.shape),
            whole((blocks, PB)),
            whole(red.shape),
            whole(tx_paths.shape),
            pl.BlockSpec((rows, PB, lanes), lambda i: (i, 0, 0)),
            pl.BlockSpec((rows, cells, pixels), lambda i: (i, 0, 0)),
        ],
        out_specs=whole((parts, PB)),
        out_shape=shaped(parts, PB),
        scratch_shapes=[
            pltpu.VMEM((tx_count, blocks, PB), F32),
            pltpu.VMEM((PB, lanes), F32),
            pltpu.VMEM((rows, blocks, PB), F32),
            pltpu.VMEM((cells, PB), F32),
        ],
        compiler_params=params(12),
        name="gradient",
    )(
        me,
        patch_cotangent.reshape(-1, 1),
        every,
        pixel_order.reshape(blocks, PB),
        red,
        tx_paths,
        slope,
        rx_paths,
    )


def on_device(slowness, tx_paths, rx_paths, traces, tap_start, pixel_order, patch_cotangent):
    tx_count, cells, _ = tx_paths.shape
    tx_size = lax.axis_size("tx")
    rx_size = lax.axis_size("rx")
    s_row = slowness.reshape(1, cells)

    delay = tx_delays(s_row, tx_paths, rx_size)
    rx_delay, window = prepare(s_row, rx_paths, traces, tap_start)
    tx_delay = lax.all_to_all(delay, "rx", 0, 0)
    slope, part = focus(tx_delay, rx_delay, window)
    part = lax.all_to_all(part, "rx", 0, 0)
    red, pair = pl.pallas_call(
        gather_sum_kernel,
        out_shape=[shaped(2 * tx_count, PB), shaped(tx_size, 2, PB)],
        compiler_params=params(4),
        name="sum_receivers",
    )(part)
    pair = lax.all_to_all(pair, "tx", 0, 0)
    spread = pl.pallas_call(
        spread_kernel,
        out_shape=shaped(rx_size, tx_count + 2, PB),
        compiler_params=params(4),
        name="sum_transmits",
    )(pair, red)
    every = lax.all_to_all(spread, "rx", 0, 0)
    me = lax.axis_index("rx").astype(jnp.int32).reshape(1)
    share = gradient(
        tx_count * tx_size,
        tx_size * rx_size,
        me,
        patch_cotangent,
        every,
        pixel_order,
        red,
        tx_paths,
        slope,
        rx_paths,
    )
    share = lax.all_to_all(share, ("tx", "rx"), 0, 0, tiled=True)
    return share.sum(0)[:cells]


def solution(mesh):
    in_specs = (
        P(),
        P("tx", None, "rx"),
        P("rx", None, None),
        P("tx", "rx", None),
        P("tx", "rx", None),
        P(),
        P(),
    )
    out_specs = P()
    return jax.shard_map(
        on_device, mesh=mesh, in_specs=in_specs, out_specs=out_specs, check_vma=False
    )
```

```python
import math

import jax
import jax.numpy as jnp
from jax import lax
from jax.experimental import pallas as pl
from jax.experimental.pallas import tpu as pltpu
from jax.sharding import PartitionSpec as P

W = 8
PB = 128
PP = 256
EPS = 1e-06
LN2 = math.log(2.0)
HALF_LOG2E = 0.5 / LN2
F32 = jnp.float32


def block_diagonal(s_row, rows, cells):
    wide = jnp.concatenate([s_row] * rows, axis=1)
    shape = (rows, rows * cells)
    owner = lax.broadcasted_iota(jnp.int32, shape, 1) // cells
    mine = owner == lax.broadcasted_iota(jnp.int32, shape, 0)
    return jnp.where(mine, jnp.broadcast_to(wide, shape), 0.0).astype(jnp.bfloat16)


def tx_delay_kernel(s_ref, path_ref, out_ref):
    rows, cells, width = path_ref.shape
    left = block_diagonal(s_ref[...].astype(F32), rows, cells)
    delay = jnp.dot(
        left, path_ref[...].reshape(rows * cells, width), preferred_element_type=F32
    )
    out_ref[...] = jnp.broadcast_to((delay * HALF_LOG2E)[None], out_ref.shape)


def prepare_kernel(s_ref, path_ref, trace_ref, start_ref, delay_ref, win_ref, sample_ref, plain_ref):
    step = pl.program_id(0)
    rows, cells, pixels = path_ref.shape
    count = trace_ref.shape[0]
    blocks = start_ref.shape[2]
    per = 128 // blocks

    @pl.when(step == 0)
    def _():
        sample_ref[...] = trace_ref[...].astype(F32)

    left = block_diagonal(s_ref[...].astype(F32), rows, cells)
    delay = jnp.dot(
        left, path_ref[...].reshape(rows * cells, pixels), preferred_element_type=F32
    )
    delay = delay * HALF_LOG2E
    for k in range(blocks):
        plain_ref[:, k, :] = delay[:, k * PB : (k + 1) * PB]
    for r in range(rows):
        delay_ref[r] = jnp.concatenate([plain_ref[r]] * per, axis=0).T

    mine = pl.ds(pl.multiple_of(step * rows, rows), rows)
    shape = (rows, 128)
    group = lax.broadcasted_iota(jnp.int32, shape, 1) // blocks
    for early in range(0, count, per):
        picks = []
        for t in range(early, early + per):
            starts = jnp.concatenate([start_ref[t, mine, :]] * per, axis=1)
            for first in range(0, W, per):
                index = starts + (group + first)
                low = index & 127
                high = index >> 7
                picked = None
                for part in range(sample_ref.shape[2] // 128):
                    source = sample_ref[t, mine, part * 128 : (part + 1) * 128]
                    got = jnp.take_along_axis(source, low, axis=1, mode="promise_in_bounds")
                    picked = got if picked is None else jnp.where(high == part, got, picked)
                picks.append(picked)
        for j in range(W):
            total = None
            for i in range(per):
                rolled = picks[i * (W // per) + j // per]
                shift = ((i - j % per) * blocks) % 128
                if shift:
                    rolled = pltpu.roll(rolled, shift, 1)
                total = rolled if total is None else jnp.where(group == i, rolled, total)
            off = j - (W - 1) / 2.0
            lanes = slice(early * blocks, early * blocks + 128)
            win_ref[:, j, lanes] = total * math.exp(-0.5 * off * off)


def focus_kernel(tx_ref, rx_ref, win_ref, slope_ref, sum_ref, tx_lane_ref, total_f_ref, total_s_ref):
    blocks, count, _ = tx_ref.shape
    rows = rx_ref.shape[0]
    per = 128 // blocks
    limit = 9.25 / LN2
    halves = count // per

    for half in range(halves):
        stack = [tx_ref[:, half * per + i, :] for i in range(per)]
        tx_lane_ref[:, half * 128 : (half + 1) * 128] = jnp.concatenate(stack, axis=0).T
    total_f_ref[...] = jnp.zeros_like(total_f_ref)
    total_s_ref[...] = jnp.zeros_like(total_s_ref)

    def horner(z, c3, c2, c1, c0):
        p1 = c3 * z + c2
        p2 = p1 * z + c1
        d2 = c3 * z + p1
        return p2 * z + c0, d2 * z + p2

    def point(tap, h):
        h = jnp.minimum(jnp.maximum(h, -limit), limit)
        m = h * (-LN2)
        s = jnp.exp2(h)
        si = jnp.exp2(-h)
        gauss = jnp.exp2(m * h)
        u = s * s
        v = si * si
        up, dup = horner(u, tap[7], tap[6], tap[5], tap[4])
        down, ddown = horner(v, tap[0], tap[1], tap[2], tap[3])
        x = s * up
        y = si * down
        both = x + y
        change = (x - y) * 0.5 + ((s * u) * dup - (si * v) * ddown)
        focused = gauss * (gauss * both)
        slope = gauss * (gauss * (change + (m + m) * both))
        return focused, slope

    def receiver(r, carry):
        for half in range(halves):
            lanes = slice(half * 128, (half + 1) * 128)
            tap = [
                jnp.broadcast_to(win_ref[r, j : j + 1, lanes], (8, 128)) for j in range(W)
            ]
            for first in range(0, PB, 8):
                here = slice(first, first + 8)
                h = tx_lane_ref[here, lanes] + rx_ref[r, here, :]
                focused, slope = point(tap, h)
                slope_ref[r, here, lanes] = slope
                total_f_ref[here, lanes] += focused
                total_s_ref[here, lanes] += slope
        return carry

    lax.fori_loop(0, rows, receiver, 0)
    for source, base in ((total_f_ref, 0), (total_s_ref, count)):
        for half in range(halves):
            turned = source[:, half * 128 : (half + 1) * 128].T
            for i in range(per):
                sum_ref[:, base + half * per + i, :] = turned[i * blocks : (i + 1) * blocks]


def gather_sum_kernel(part_ref, red_ref, rep_ref):
    total = part_ref[0]
    for i in range(1, part_ref.shape[0]):
        total = total + part_ref[i]
    red_ref[...] = total
    beam = total[0 : total.shape[0] // 2]
    coherent = jnp.sum(beam, axis=0, keepdims=True)
    power = jnp.sum(beam * beam, axis=0, keepdims=True)
    pair = jnp.concatenate([coherent, power], axis=0)
    rep_ref[...] = jnp.broadcast_to(pair[None], rep_ref.shape)


def spread_kernel(pair_ref, red_ref, out_ref):
    pair = pair_ref[0]
    for i in range(1, pair_ref.shape[0]):
        pair = pair + pair_ref[i]
    count = red_ref.shape[0] // 2
    out_ref[:, 0:count, :] = jnp.broadcast_to(
        red_ref[0:count, :][None], (out_ref.shape[0], count, PB)
    )
    out_ref[:, count : count + 2, :] = jnp.broadcast_to(
        pair[None], (out_ref.shape[0], 2, PB)
    )


def patch_scales(total_tx, cot_ref, ids, coherent, power):
    patches = cot_ref.shape[0]
    square = coherent * coherent
    sums = []
    for field in (square, power):
        rows = [
            jnp.sum(jnp.where(ids == q, field, 0.0), axis=0, keepdims=True)
            for q in range(patches)
        ]
        sums.append(jnp.sum(jnp.concatenate(rows, axis=0), axis=1, keepdims=True))
    numer, power_sum = sums
    denom = total_tx * power_sum
    cot = jnp.zeros_like(numer)
    row = lax.broadcasted_iota(jnp.int32, cot.shape, 0)
    for q in range(patches):
        cot = jnp.where(row == q, cot_ref[q], cot)
    value_n = -2.0 * (cot / (numer + EPS))
    value_d = 2.0 * (cot * total_tx / (denom + EPS))
    scale_n = jnp.zeros_like(square)
    scale_d = jnp.zeros_like(square)
    for q in range(patches):
        inside = ids == q
        scale_n = jnp.where(inside, value_n[q : q + 1, :], scale_n)
        scale_d = jnp.where(inside, value_d[q : q + 1, :], scale_d)
    return scale_n, scale_d


def gradient_kernel(
    total_tx,
    cot_ref,
    all_ref,
    ids_ref,
    red_ref,
    tx_path_ref,
    slope_ref,
    path_ref,
    out_ref,
    bg_ref,
    bg_lane_ref,
    grad_ref,
    acc_ref,
):
    step = pl.program_id(0)
    rows, cells, _ = path_ref.shape
    blocks = all_ref.shape[0]
    count = red_ref.shape[0] // 2
    per = 128 // blocks

    @pl.when(step == 0)
    def _():
        coherent = all_ref[:, count, :]
        power = all_ref[:, count + 1, :]
        scale_n, scale_d = patch_scales(total_tx, cot_ref, ids_ref[...] // PP, coherent, power)
        common = coherent * scale_n
        for t in range(count):
            bg_ref[t] = common + all_ref[:, t, :] * scale_d
        for half in range(count // per):
            stack = [bg_ref[half * per + i] for i in range(per)]
            bg_lane_ref[:, half * 128 : (half + 1) * 128] = jnp.concatenate(stack, axis=0).T
        acc = jnp.zeros((cells, PB), F32)
        me = lax.axis_index("rx")
        for t in range(count):
            own = bg_ref[t, pl.ds(me, 1), :] * red_ref[count + t : count + t + 1, :]
            acc = acc + tx_path_ref[t].astype(F32) * own
        acc_ref[...] = acc

    acc = [acc_ref[...], jnp.zeros((cells, PB), F32)]
    for r in range(rows):
        grad = None
        for half in range(count // per):
            lanes = slice(half * 128, (half + 1) * 128)
            term = slope_ref[r, :, lanes] * bg_lane_ref[:, lanes]
            grad = term if grad is None else grad + term
        grad = grad.T
        total = grad[0:blocks]
        for i in range(1, per):
            total = total + grad[i * blocks : (i + 1) * blocks]
        grad_ref[r] = total
        for k in range(blocks):
            paths = path_ref[r, :, k * PB : (k + 1) * PB].astype(F32)
            acc[k % 2] = acc[k % 2] + paths * grad_ref[r, k : k + 1, :]
    acc = acc[0] + acc[1]
    acc_ref[...] = acc

    @pl.when(step == pl.num_programs(0) - 1)
    def _():
        ones = jnp.ones((8, PB), F32)
        row = lax.dot_general(
            ones,
            acc,
            (((1,), (1,)), ((), ())),
            precision=lax.Precision.HIGHEST,
            preferred_element_type=F32,
        )
        row = jnp.concatenate([row] * (PB // cells), axis=1)
        out_ref[...] = jnp.broadcast_to(row[0:1, :], out_ref.shape)


def params(megabytes):
    return pltpu.CompilerParams(vmem_limit_bytes=megabytes * 1024 * 1024)


def whole(shape):
    return pl.BlockSpec(shape, lambda *_: (0,) * len(shape))


def shaped(*shape):
    return jax.ShapeDtypeStruct(shape, F32)


def in_hbm(array):
    return pltpu.with_memory_space_constraint(array, pltpu.HBM)


def tx_delays(s_row, tx_paths, rx_size):
    tx_count, _, own_pixels = tx_paths.shape
    return pl.pallas_call(
        tx_delay_kernel,
        out_shape=shaped(rx_size, tx_count, own_pixels),
        compiler_params=params(4),
        name="tx_delay",
    )(in_hbm(s_row), in_hbm(tx_paths))


def prepare(s_row, rx_paths, traces, tap_start):
    rx_count, cells, pixels = rx_paths.shape
    tx_count, _, samples = traces.shape
    blocks = pixels // PB
    rows = 8
    return pl.pallas_call(
        prepare_kernel,
        grid=(rx_count // rows,),
        in_specs=[
            whole((1, cells)),
            pl.BlockSpec((rows, cells, pixels), lambda i: (i, 0, 0)),
            whole((tx_count, rx_count, samples)),
            whole((tx_count, rx_count, blocks)),
        ],
        out_specs=[
            pl.BlockSpec((rows, PB, 128), lambda i: (i, 0, 0)),
            pl.BlockSpec((rows, W, tx_count * blocks), lambda i: (i, 0, 0)),
        ],
        out_shape=[shaped(rx_count, PB, 128), shaped(rx_count, W, tx_count * blocks)],
        scratch_shapes=[
            pltpu.VMEM((tx_count, rx_count, samples), F32),
            pltpu.VMEM((rows, blocks, PB), F32),
        ],
        compiler_params=params(12),
        name="prepare",
    )(in_hbm(s_row), in_hbm(rx_paths), in_hbm(traces), in_hbm(tap_start))


def focus(tx_delay, rx_delay, window):
    blocks, tx_count, _ = tx_delay.shape
    rx_count = rx_delay.shape[0]
    lanes = tx_count * blocks
    return pl.pallas_call(
        focus_kernel,
        out_shape=[shaped(rx_count, PB, lanes), shaped(blocks, 2 * tx_count, PB)],
        scratch_shapes=[pltpu.VMEM((PB, lanes), F32)] * 3,
        compiler_params=params(12),
        name="focus",
    )(tx_delay, rx_delay, window)


def gradient(total_tx, parts, patch_cotangent, every, pixel_order, red, tx_paths, slope, rx_paths):
    rx_count, cells, pixels = rx_paths.shape
    blocks = pixels // PB
    tx_count = tx_paths.shape[0]
    lanes = tx_count * blocks
    rows = 4
    return pl.pallas_call(
        lambda *refs: gradient_kernel(total_tx, *refs),
        grid=(rx_count // rows,),
        in_specs=[
            pl.BlockSpec(memory_space=pltpu.SMEM),
            whole(every.shape),
            whole((blocks, PB)),
            whole(red.shape),
            whole(tx_paths.shape),
            pl.BlockSpec((rows, PB, lanes), lambda i: (i, 0, 0)),
            pl.BlockSpec((rows, cells, pixels), lambda i: (i, 0, 0)),
        ],
        out_specs=whole((parts, PB)),
        out_shape=shaped(parts, PB),
        scratch_shapes=[
            pltpu.VMEM((tx_count, blocks, PB), F32),
            pltpu.VMEM((PB, lanes), F32),
            pltpu.VMEM((rows, blocks, PB), F32),
            pltpu.VMEM((cells, PB), F32),
        ],
        compiler_params=params(12),
        name="gradient",
    )(
        patch_cotangent,
        every,
        pixel_order.reshape(blocks, PB),
        red,
        tx_paths,
        slope,
        rx_paths,
    )


def on_device(slowness, tx_paths, rx_paths, traces, tap_start, pixel_order, patch_cotangent):
    tx_count, cells, _ = tx_paths.shape
    tx_size = lax.axis_size("tx")
    rx_size = lax.axis_size("rx")
    s_row = slowness.reshape(1, cells)

    delay = tx_delays(s_row, tx_paths, rx_size)
    rx_delay, window = prepare(s_row, rx_paths, traces, tap_start)
    tx_delay = lax.all_to_all(delay, "rx", 0, 0)
    slope, part = focus(tx_delay, rx_delay, window)
    part = lax.all_to_all(part, "rx", 0, 0)
    red, pair = pl.pallas_call(
        gather_sum_kernel,
        out_shape=[shaped(2 * tx_count, PB), shaped(tx_size, 2, PB)],
        compiler_params=params(4),
        name="sum_receivers",
    )(part)
    pair = lax.all_to_all(pair, "tx", 0, 0)
    spread = pl.pallas_call(
        spread_kernel,
        out_shape=shaped(rx_size, tx_count + 2, PB),
        compiler_params=params(4),
        name="sum_transmits",
    )(pair, red)
    every = lax.all_to_all(spread, "rx", 0, 0)
    share = gradient(
        tx_count * tx_size,
        tx_size * rx_size,
        patch_cotangent,
        every,
        pixel_order,
        red,
        tx_paths,
        slope,
        rx_paths,
    )
    share = lax.all_to_all(share, ("tx", "rx"), 0, 0, tiled=True)
    return share.sum(0)[:cells]


def solution(mesh):
    in_specs = (
        P(),
        P("tx", None, "rx"),
        P("rx", None, None),
        P("tx", "rx", None),
        P("tx", "rx", None),
        P(),
        P(),
    )
    out_specs = P()
    return jax.shard_map(
        on_device, mesh=mesh, in_specs=in_specs, out_specs=out_specs, check_vma=False
    )
```

```python
import math

import jax
import jax.numpy as jnp
from jax import lax
from jax.experimental import pallas as pl
from jax.experimental.pallas import tpu as pltpu
from jax.sharding import PartitionSpec as P

W = 8
PB = 128
PP = 256
EPS = 1e-06
LN2 = math.log(2.0)
HALF_LOG2E = 0.5 / LN2
F32 = jnp.float32


def block_diagonal(s_row, rows, cells):
    wide = jnp.concatenate([s_row] * rows, axis=1)
    shape = (rows, rows * cells)
    owner = lax.broadcasted_iota(jnp.int32, shape, 1) // cells
    mine = owner == lax.broadcasted_iota(jnp.int32, shape, 0)
    return jnp.where(mine, jnp.broadcast_to(wide, shape), 0.0).astype(jnp.bfloat16)


def tx_delay_kernel(s_ref, path_ref, out_ref):
    rows, cells, width = path_ref.shape
    left = block_diagonal(s_ref[...].astype(F32), rows, cells)
    delay = jnp.dot(
        left, path_ref[...].reshape(rows * cells, width), preferred_element_type=F32
    )
    out_ref[...] = jnp.broadcast_to((delay * HALF_LOG2E)[None], out_ref.shape)


def prepare_kernel(s_ref, path_ref, trace_ref, start_ref, delay_ref, win_ref, sample_ref, plain_ref):
    step = pl.program_id(0)
    rows, cells, pixels = path_ref.shape
    count = trace_ref.shape[0]
    blocks = start_ref.shape[2]
    per = 128 // blocks

    @pl.when(step == 0)
    def _():
        sample_ref[...] = trace_ref[...].astype(F32)

    left = block_diagonal(s_ref[...].astype(F32), rows, cells)
    delay = jnp.dot(
        left, path_ref[...].reshape(rows * cells, pixels), preferred_element_type=F32
    )
    delay = delay * HALF_LOG2E
    for k in range(blocks):
        plain_ref[:, k, :] = delay[:, k * PB : (k + 1) * PB]
    for r in range(rows):
        delay_ref[r] = jnp.concatenate([plain_ref[r]] * per, axis=0).T

    mine = pl.ds(pl.multiple_of(step * rows, rows), rows)
    shape = (rows, 128)
    group = lax.broadcasted_iota(jnp.int32, shape, 1) // blocks
    for early in range(0, count, per):
        picks = []
        for t in range(early, early + per):
            starts = jnp.concatenate([start_ref[t, mine, :]] * per, axis=1)
            for first in range(0, W, per):
                index = starts + (group + first)
                low = index & 127
                high = index >> 7
                picked = None
                for part in range(sample_ref.shape[2] // 128):
                    source = sample_ref[t, mine, part * 128 : (part + 1) * 128]
                    got = jnp.take_along_axis(source, low, axis=1, mode="promise_in_bounds")
                    picked = got if picked is None else jnp.where(high == part, got, picked)
                picks.append(picked)
        for j in range(W):
            total = None
            for i in range(per):
                rolled = picks[i * (W // per) + j // per]
                shift = ((i - j % per) * blocks) % 128
                if shift:
                    rolled = pltpu.roll(rolled, shift, 1)
                total = rolled if total is None else jnp.where(group == i, rolled, total)
            off = j - (W - 1) / 2.0
            lanes = slice(early * blocks, early * blocks + 128)
            win_ref[:, j, lanes] = total * math.exp(-0.5 * off * off)


def focus_kernel(
    tx_ref,
    rx_ref,
    win_ref,
    path_ref,
    slope_ref,
    keep_ref,
    give_ref,
    path_copy_ref,
    tx_lane_ref,
    total_f_ref,
    total_s_ref,
    turned_ref,
    copied,
):
    fetch = pltpu.make_async_copy(path_ref, path_copy_ref, copied)
    fetch.start()
    blocks, count, _ = tx_ref.shape
    rows = rx_ref.shape[0]
    per = 128 // blocks
    limit = 9.25 / LN2
    halves = count // per

    for half in range(halves):
        stack = [tx_ref[:, half * per + i, :] for i in range(per)]
        tx_lane_ref[:, half * 128 : (half + 1) * 128] = jnp.concatenate(stack, axis=0).T
    total_f_ref[...] = jnp.zeros_like(total_f_ref)
    total_s_ref[...] = jnp.zeros_like(total_s_ref)

    def horner(z, c3, c2, c1, c0):
        p1 = c3 * z + c2
        p2 = p1 * z + c1
        d2 = c3 * z + p1
        return p2 * z + c0, d2 * z + p2

    def point(tap, h):
        h = jnp.minimum(jnp.maximum(h, -limit), limit)
        m = h * (-LN2)
        s = jnp.exp2(h)
        si = jnp.exp2(-h)
        gauss = jnp.exp2(m * h)
        u = s * s
        v = si * si
        up, dup = horner(u, tap[7], tap[6], tap[5], tap[4])
        down, ddown = horner(v, tap[0], tap[1], tap[2], tap[3])
        x = s * up
        y = si * down
        both = x + y
        change = (x - y) * 0.5 + ((s * u) * dup - (si * v) * ddown)
        focused = gauss * (gauss * both)
        slope = gauss * (gauss * (change + (m + m) * both))
        return focused, slope

    def receiver(r, carry):
        for half in range(halves):
            lanes = slice(half * 128, (half + 1) * 128)
            tap = [
                jnp.broadcast_to(win_ref[r, j : j + 1, lanes], (8, 128)) for j in range(W)
            ]
            for first in range(0, PB, 8):
                here = slice(first, first + 8)
                h = tx_lane_ref[here, lanes] + rx_ref[r, here, :]
                focused, slope = point(tap, h)
                slope_ref[r, here, lanes] = slope
                total_f_ref[here, lanes] += focused
                total_s_ref[here, lanes] += slope
        return carry

    lax.fori_loop(0, rows, receiver, 0)
    mine = lax.axis_index("rx") % 2
    for source, base in ((total_f_ref, 0), (total_s_ref, count)):
        for half in range(halves):
            turned_ref[...] = source[:, half * 128 : (half + 1) * 128].T
            for i in range(per):
                row = base + half * per + i
                even = turned_ref[pl.ds(i * blocks, blocks // 2, stride=2), :]
                odd = turned_ref[pl.ds(i * blocks + 1, blocks // 2, stride=2), :]
                keep_ref[:, row, :] = jnp.where(mine == 0, even, odd)
                give_ref[:, row, :] = jnp.where(mine == 0, odd, even)
    fetch.wait()


def pair_sum_kernel(keep_ref, got_ref, out_ref):
    out_ref[...] = keep_ref[...] + got_ref[...]


def gather_sum_kernel(part_ref, red_ref, rep_ref):
    total = part_ref[0]
    for i in range(1, part_ref.shape[0]):
        total = total + part_ref[i]
    red_ref[...] = total
    beam = total[0 : total.shape[0] // 2]
    coherent = jnp.sum(beam, axis=0, keepdims=True)
    power = jnp.sum(beam * beam, axis=0, keepdims=True)
    pair = jnp.concatenate([coherent, power], axis=0)
    rep_ref[...] = jnp.broadcast_to(pair[None], rep_ref.shape)


def spread_kernel(pair_ref, red_ref, out_ref):
    pair = pair_ref[0]
    for i in range(1, pair_ref.shape[0]):
        pair = pair + pair_ref[i]
    count = red_ref.shape[0] // 2
    out_ref[:, 0:count, :] = jnp.broadcast_to(
        red_ref[0:count, :][None], (out_ref.shape[0], count, PB)
    )
    out_ref[:, count : count + 2, :] = jnp.broadcast_to(
        pair[None], (out_ref.shape[0], 2, PB)
    )


def patch_scales(total_tx, cot_ref, ids, coherent, power):
    patches = cot_ref.shape[0]
    square = coherent * coherent
    sums = []
    for field in (square, power):
        rows = [
            jnp.sum(jnp.where(ids == q, field, 0.0), axis=0, keepdims=True)
            for q in range(patches)
        ]
        sums.append(jnp.sum(jnp.concatenate(rows, axis=0), axis=1, keepdims=True))
    numer, power_sum = sums
    denom = total_tx * power_sum
    cot = jnp.zeros_like(numer)
    row = lax.broadcasted_iota(jnp.int32, cot.shape, 0)
    for q in range(patches):
        cot = jnp.where(row == q, cot_ref[q], cot)
    value_n = -2.0 * (cot / (numer + EPS))
    value_d = 2.0 * (cot * total_tx / (denom + EPS))
    scale_n = jnp.zeros_like(square)
    scale_d = jnp.zeros_like(square)
    for q in range(patches):
        inside = ids == q
        scale_n = jnp.where(inside, value_n[q : q + 1, :], scale_n)
        scale_d = jnp.where(inside, value_d[q : q + 1, :], scale_d)
    return scale_n, scale_d


def gradient_kernel(
    total_tx,
    cot_ref,
    here_ref,
    there_ref,
    ids_ref,
    red_ref,
    tx_path_ref,
    slope_ref,
    path_ref,
    out_ref,
    all_ref,
    bg_ref,
    bg_lane_ref,
    grad_ref,
):
    rows, cells, _ = path_ref.shape
    pairs = here_ref.shape[0]
    blocks = 2 * pairs
    count = red_ref.shape[0] // 2
    per = 128 // blocks
    together = grad_ref.shape[0]
    me = lax.axis_index("rx")

    for row in range(count + 2):
        here = here_ref[:, row, :]
        there = there_ref[:, row, :]
        all_ref[row, pl.ds(0, pairs, stride=2), :] = jnp.where(me % 2 == 0, here, there)
        all_ref[row, pl.ds(1, pairs, stride=2), :] = jnp.where(me % 2 == 0, there, here)
    coherent = all_ref[count]
    power = all_ref[count + 1]
    scale_n, scale_d = patch_scales(total_tx, cot_ref, ids_ref[...] // PP, coherent, power)
    common = coherent * scale_n
    for t in range(count):
        bg_ref[t] = common + all_ref[t] * scale_d
    for half in range(count // per):
        stack = [bg_ref[half * per + i] for i in range(per)]
        bg_lane_ref[:, half * 128 : (half + 1) * 128] = jnp.concatenate(stack, axis=0).T
    start = jnp.zeros((cells, PB), F32)
    for t in range(count):
        own = bg_ref[t, pl.ds(me, 1), :] * red_ref[count + t : count + t + 1, :]
        start = start + tx_path_ref[t].astype(F32) * own

    def receivers(step, acc):
        acc = list(acc)
        for i in range(together):
            r = step * together + i
            grad = None
            for half in range(count // per):
                lanes = slice(half * 128, (half + 1) * 128)
                term = slope_ref[r, :, lanes] * bg_lane_ref[:, lanes]
                grad = term if grad is None else grad + term
            grad = grad.T
            total = grad[0:blocks]
            for group in range(1, per):
                total = total + grad[group * blocks : (group + 1) * blocks]
            grad_ref[i] = total
            for k in range(blocks):
                paths = path_ref[r, :, k * PB : (k + 1) * PB].astype(F32)
                acc[k % 2] = acc[k % 2] + paths * grad_ref[i, k : k + 1, :]
        return tuple(acc)

    acc = lax.fori_loop(0, rows // together, receivers, (start, jnp.zeros_like(start)))
    row = lax.dot_general(
        jnp.ones((8, PB), F32),
        acc[0] + acc[1],
        (((1,), (1,)), ((), ())),
        precision=lax.Precision.HIGHEST,
        preferred_element_type=F32,
    )
    row = jnp.concatenate([row] * (PB // cells), axis=1)
    out_ref[...] = jnp.broadcast_to(row[0:1, :], out_ref.shape)


def params(megabytes):
    return pltpu.CompilerParams(vmem_limit_bytes=megabytes * 1024 * 1024)


def whole(shape):
    return pl.BlockSpec(shape, lambda *_: (0,) * len(shape))


def shaped(*shape):
    return jax.ShapeDtypeStruct(shape, F32)


def in_hbm(array):
    return pltpu.with_memory_space_constraint(array, pltpu.HBM)


def tx_delays(s_row, tx_paths, rx_size):
    tx_count, _, own_pixels = tx_paths.shape
    return pl.pallas_call(
        tx_delay_kernel,
        out_shape=shaped(rx_size, tx_count, own_pixels),
        compiler_params=params(4),
        name="tx_delay",
    )(in_hbm(s_row), in_hbm(tx_paths))


def prepare(s_row, rx_paths, traces, tap_start):
    rx_count, cells, pixels = rx_paths.shape
    tx_count, _, samples = traces.shape
    blocks = pixels // PB
    rows = 8
    return pl.pallas_call(
        prepare_kernel,
        grid=(rx_count // rows,),
        in_specs=[
            whole((1, cells)),
            pl.BlockSpec((rows, cells, pixels), lambda i: (i, 0, 0)),
            whole((tx_count, rx_count, samples)),
            whole((tx_count, rx_count, blocks)),
        ],
        out_specs=[
            pl.BlockSpec((rows, PB, 128), lambda i: (i, 0, 0)),
            pl.BlockSpec((rows, W, tx_count * blocks), lambda i: (i, 0, 0)),
        ],
        out_shape=[shaped(rx_count, PB, 128), shaped(rx_count, W, tx_count * blocks)],
        scratch_shapes=[
            pltpu.VMEM((tx_count, rx_count, samples), F32),
            pltpu.VMEM((rows, blocks, PB), F32),
        ],
        compiler_params=params(12),
        name="prepare",
    )(in_hbm(s_row), in_hbm(rx_paths), in_hbm(traces), in_hbm(tap_start))


def focus(tx_delay, rx_delay, window, rx_paths):
    blocks, tx_count, _ = tx_delay.shape
    rx_count = rx_delay.shape[0]
    lanes = tx_count * blocks
    vmem = pl.BlockSpec(memory_space=pltpu.VMEM)
    return pl.pallas_call(
        focus_kernel,
        in_specs=[vmem, vmem, vmem, pl.BlockSpec(memory_space=pl.ANY)],
        out_specs=[vmem] * 4,
        out_shape=[
            shaped(rx_count, PB, lanes),
            shaped(blocks // 2, 2 * tx_count, PB),
            shaped(blocks // 2, 2 * tx_count, PB),
            jax.ShapeDtypeStruct(rx_paths.shape, rx_paths.dtype),
        ],
        scratch_shapes=[pltpu.VMEM((PB, lanes), F32)] * 3
        + [pltpu.VMEM((128, PB), F32), pltpu.SemaphoreType.DMA],
        compiler_params=params(20),
        name="focus",
    )(tx_delay, rx_delay, window, in_hbm(rx_paths))


def gradient(total_tx, parts, patch_cotangent, here, there, pixel_order, red, tx_paths, slope, rx_paths):
    rx_count = rx_paths.shape[0]
    blocks = 2 * here.shape[0]
    tx_count = tx_paths.shape[0]
    lanes = tx_count * blocks
    together = 4
    vmem = pl.BlockSpec(memory_space=pltpu.VMEM)
    return pl.pallas_call(
        lambda *refs: gradient_kernel(total_tx, *refs),
        in_specs=[pl.BlockSpec(memory_space=pltpu.SMEM)] + [vmem] * 7,
        out_specs=vmem,
        out_shape=shaped(parts, PB),
        scratch_shapes=[
            pltpu.VMEM((tx_count + 2, blocks, PB), F32),
            pltpu.VMEM((tx_count, blocks, PB), F32),
            pltpu.VMEM((PB, lanes), F32),
            pltpu.VMEM((together, blocks, PB), F32),
        ],
        compiler_params=params(20),
        name="gradient",
    )(
        patch_cotangent,
        here,
        there,
        pixel_order.reshape(blocks, PB),
        red,
        tx_paths,
        slope,
        rx_paths,
    )


def on_device(slowness, tx_paths, rx_paths, traces, tap_start, pixel_order, patch_cotangent):
    tx_count, cells, _ = tx_paths.shape
    tx_size = lax.axis_size("tx")
    rx_size = lax.axis_size("rx")
    pairs = rx_size // 2
    s_row = slowness.reshape(1, cells)
    partner = [(i, i ^ 1) for i in range(rx_size)]
    same_core = [list(range(core, rx_size, 2)) for core in range(2)]

    def between_chips(array):
        return lax.all_to_all(array, "rx", 0, 0, axis_index_groups=same_core)

    delay = tx_delays(s_row, tx_paths, rx_size)
    rx_delay, window = prepare(s_row, rx_paths, traces, tap_start)
    tx_delay = lax.all_to_all(delay, "rx", 0, 0)
    slope, keep, give, path_copy = focus(tx_delay, rx_delay, window, rx_paths)
    got = lax.ppermute(give, "rx", partner)
    part = pl.pallas_call(
        pair_sum_kernel,
        out_shape=shaped(*keep.shape),
        compiler_params=params(4),
        name="sum_cores",
    )(keep, got)
    part = between_chips(part)
    red, pair = pl.pallas_call(
        gather_sum_kernel,
        out_shape=[shaped(2 * tx_count, PB), shaped(tx_size, 2, PB)],
        compiler_params=params(4),
        name="sum_receivers",
    )(part)
    pair = lax.all_to_all(pair, "tx", 0, 0)
    spread = pl.pallas_call(
        spread_kernel,
        out_shape=shaped(pairs, tx_count + 2, PB),
        compiler_params=params(4),
        name="sum_transmits",
    )(pair, red)
    here = between_chips(spread)
    there = lax.ppermute(here, "rx", partner)
    share = gradient(
        tx_count * tx_size,
        tx_size * rx_size,
        patch_cotangent,
        here,
        there,
        pixel_order,
        red,
        tx_paths,
        slope,
        path_copy,
    )
    share = lax.all_to_all(share, ("tx", "rx"), 0, 0, tiled=True)
    return share.sum(0)[:cells]


def solution(mesh):
    in_specs = (
        P(),
        P("tx", None, "rx"),
        P("rx", None, None),
        P("tx", "rx", None),
        P("tx", "rx", None),
        P(),
        P(),
    )
    out_specs = P()
    return jax.shard_map(
        on_device, mesh=mesh, in_specs=in_specs, out_specs=out_specs, check_vma=False
    )
```

```python
import math

import jax
import jax.numpy as jnp
from jax import lax
from jax.experimental import pallas as pl
from jax.experimental.pallas import tpu as pltpu
from jax.sharding import PartitionSpec as P

W = 8
PB = 128
PP = 256
EPS = 1e-06
LN2 = math.log(2.0)
HALF_LOG2E = 0.5 / LN2
F32 = jnp.float32


def block_diagonal(s_row, rows, cells):
    wide = jnp.concatenate([s_row] * rows, axis=1)
    shape = (rows, rows * cells)
    owner = lax.broadcasted_iota(jnp.int32, shape, 1) // cells
    mine = owner == lax.broadcasted_iota(jnp.int32, shape, 0)
    return jnp.where(mine, jnp.broadcast_to(wide, shape), 0.0).astype(jnp.bfloat16)


def tx_delay_kernel(s_hbm, path_hbm, out_ref, s_ref, path_ref, copied):
    fetches = [
        pltpu.make_async_copy(s_hbm, s_ref, copied.at[0]),
        pltpu.make_async_copy(path_hbm, path_ref, copied.at[1]),
    ]
    for fetch in fetches:
        fetch.start()
    for fetch in fetches:
        fetch.wait()
    rows, cells, width = path_ref.shape
    left = block_diagonal(s_ref[...].astype(F32), rows, cells)
    delay = jnp.dot(
        left, path_ref[...].reshape(rows * cells, width), preferred_element_type=F32
    )
    out_ref[...] = jnp.broadcast_to((delay * HALF_LOG2E)[None], out_ref.shape)


def prepare_kernel(s_ref, path_ref, trace_ref, start_ref, delay_ref, win_ref, sample_ref, plain_ref):
    step = pl.program_id(0)
    rows, cells, pixels = path_ref.shape
    count = trace_ref.shape[0]
    blocks = start_ref.shape[2]
    per = 128 // blocks

    @pl.when(step == 0)
    def _():
        sample_ref[...] = trace_ref[...].astype(F32)

    left = block_diagonal(s_ref[...].astype(F32), rows, cells)
    delay = jnp.dot(
        left, path_ref[...].reshape(rows * cells, pixels), preferred_element_type=F32
    )
    delay = delay * HALF_LOG2E
    for k in range(blocks):
        plain_ref[:, k, :] = delay[:, k * PB : (k + 1) * PB]
    for r in range(rows):
        delay_ref[r] = jnp.concatenate([plain_ref[r]] * per, axis=0).T

    mine = pl.ds(pl.multiple_of(step * rows, rows), rows)
    shape = (rows, 128)
    group = lax.broadcasted_iota(jnp.int32, shape, 1) // blocks
    for early in range(0, count, per):
        picks = []
        for t in range(early, early + per):
            starts = jnp.concatenate([start_ref[t, mine, :]] * per, axis=1)
            for first in range(0, W, per):
                index = starts + (group + first)
                low = index & 127
                high = index >> 7
                picked = None
                for part in range(sample_ref.shape[2] // 128):
                    source = sample_ref[t, mine, part * 128 : (part + 1) * 128]
                    got = jnp.take_along_axis(source, low, axis=1, mode="promise_in_bounds")
                    picked = got if picked is None else jnp.where(high == part, got, picked)
                picks.append(picked)
        for j in range(W):
            total = None
            for i in range(per):
                rolled = picks[i * (W // per) + j // per]
                shift = ((i - j % per) * blocks) % 128
                if shift:
                    rolled = pltpu.roll(rolled, shift, 1)
                total = rolled if total is None else jnp.where(group == i, rolled, total)
            off = j - (W - 1) / 2.0
            lanes = slice(early * blocks, early * blocks + 128)
            win_ref[:, j, lanes] = total * math.exp(-0.5 * off * off)


def focus_kernel(
    tx_ref,
    rx_ref,
    win_ref,
    path_ref,
    slope_ref,
    keep_ref,
    give_ref,
    path_copy_ref,
    tx_lane_ref,
    total_f_ref,
    total_s_ref,
    turned_ref,
    copied,
):
    fetch = pltpu.make_async_copy(path_ref, path_copy_ref, copied)
    fetch.start()
    blocks, count, _ = tx_ref.shape
    rows = rx_ref.shape[0]
    per = 128 // blocks
    limit = 9.25 / LN2
    halves = count // per

    for half in range(halves):
        stack = [tx_ref[:, half * per + i, :] for i in range(per)]
        tx_lane_ref[:, half * 128 : (half + 1) * 128] = jnp.concatenate(stack, axis=0).T
    total_f_ref[...] = jnp.zeros_like(total_f_ref)
    total_s_ref[...] = jnp.zeros_like(total_s_ref)

    def horner(z, c3, c2, c1, c0):
        p1 = c3 * z + c2
        p2 = p1 * z + c1
        d2 = c3 * z + p1
        return p2 * z + c0, d2 * z + p2

    def point(tap, h):
        h = jnp.minimum(jnp.maximum(h, -limit), limit)
        m = h * (-LN2)
        s = jnp.exp2(h)
        si = jnp.exp2(-h)
        gauss = jnp.exp2(m * h)
        u = s * s
        v = si * si
        up, dup = horner(u, tap[7], tap[6], tap[5], tap[4])
        down, ddown = horner(v, tap[0], tap[1], tap[2], tap[3])
        x = s * up
        y = si * down
        both = x + y
        change = (x - y) * 0.5 + ((s * u) * dup - (si * v) * ddown)
        focused = gauss * (gauss * both)
        slope = gauss * (gauss * (change + (m + m) * both))
        return focused, slope

    def receivers(step, carry):
        for half in range(halves):
            lanes = slice(half * 128, (half + 1) * 128)
            taps = [
                [
                    jnp.broadcast_to(win_ref[2 * step + i, j : j + 1, lanes], (8, 128))
                    for j in range(W)
                ]
                for i in range(2)
            ]
            for first in range(0, PB, 8):
                here = slice(first, first + 8)
                total_f = total_f_ref[here, lanes]
                total_s = total_s_ref[here, lanes]
                for i in range(2):
                    h = tx_lane_ref[here, lanes] + rx_ref[2 * step + i, here, :]
                    focused, slope = point(taps[i], h)
                    slope_ref[2 * step + i, here, lanes] = slope
                    total_f = total_f + focused
                    total_s = total_s + slope
                total_f_ref[here, lanes] = total_f
                total_s_ref[here, lanes] = total_s
        return carry

    lax.fori_loop(0, rows // 2, receivers, 0)
    mine = lax.axis_index("rx") % 2
    for source, base in ((total_f_ref, 0), (total_s_ref, count)):
        for half in range(halves):
            turned_ref[...] = source[:, half * 128 : (half + 1) * 128].T
            for i in range(per):
                row = base + half * per + i
                even = turned_ref[pl.ds(i * blocks, blocks // 2, stride=2), :]
                odd = turned_ref[pl.ds(i * blocks + 1, blocks // 2, stride=2), :]
                keep_ref[:, row, :] = jnp.where(mine == 0, even, odd)
                give_ref[:, row, :] = jnp.where(mine == 0, odd, even)
    fetch.wait()


def pair_sum_kernel(keep_ref, got_ref, out_ref):
    out_ref[...] = keep_ref[...] + got_ref[...]


def gather_sum_kernel(part_ref, beam_ref, slope_ref):
    total = part_ref[0]
    for i in range(1, part_ref.shape[0]):
        total = total + part_ref[i]
    count = beam_ref.shape[0]
    beam_ref[...] = total[0:count]
    slope_ref[...] = total[count : 2 * count]


def square_kernel(here_ref, there_ref, out_ref):
    rows = []
    for ref in (here_ref, there_ref):
        beam = ref[...]
        rows.append(jnp.sum(beam, axis=0, keepdims=True))
        rows.append(jnp.sum(beam * beam, axis=0, keepdims=True))
    out_ref[...] = jnp.broadcast_to(jnp.concatenate(rows, axis=0)[None], out_ref.shape)


def spread_kernel(pair_ref, here_ref, there_ref, out_ref):
    even_core = lax.axis_index("rx") % 2 == 0
    total = pair_ref[0]
    for i in range(1, pair_ref.shape[0]):
        total = total + pair_ref[i]
    even = jnp.where(even_core, total[0:2], total[2:4])
    odd = jnp.where(even_core, total[2:4], total[0:2])
    here = here_ref[...]
    there = there_ref[...]
    fields = [
        jnp.where(even_core, here, there),
        jnp.where(even_core, there, here),
        jnp.concatenate([even, odd], axis=0),
    ]
    group = 0
    for field in fields:
        for first in range(0, field.shape[0], 4):
            block = field[first : first + 4]
            out_ref[:, group] = jnp.broadcast_to(block[None], (out_ref.shape[0], 4, PB))
            group += 1


def total_kernel(share_ref, out_ref):
    out_ref[...] = jnp.sum(share_ref[...], axis=0)[0 : out_ref.shape[0]]


def patch_scales(total_tx, cot_ref, ids, coherent, power):
    patches = cot_ref.shape[0]
    square = coherent * coherent
    sums = []
    for field in (square, power):
        rows = [
            jnp.sum(jnp.where(ids == q, field, 0.0), axis=0, keepdims=True)
            for q in range(patches)
        ]
        sums.append(jnp.sum(jnp.concatenate(rows, axis=0), axis=1, keepdims=True))
    numer, power_sum = sums
    denom = total_tx * power_sum
    cot = jnp.zeros_like(numer)
    row = lax.broadcasted_iota(jnp.int32, cot.shape, 0)
    for q in range(patches):
        cot = jnp.where(row == q, cot_ref[q], cot)
    value_n = -2.0 * (cot / (numer + EPS))
    value_d = 2.0 * (cot * total_tx / (denom + EPS))
    scale_n = jnp.zeros_like(square)
    scale_d = jnp.zeros_like(square)
    for q in range(patches):
        inside = ids == q
        scale_n = jnp.where(inside, value_n[q : q + 1, :], scale_n)
        scale_d = jnp.where(inside, value_d[q : q + 1, :], scale_d)
    return scale_n, scale_d


def gradient_kernel(
    total_tx,
    cot_ref,
    every_ref,
    ids_ref,
    slope_sum_ref,
    tx_path_ref,
    slope_ref,
    path_ref,
    out_ref,
    all_ref,
    bg_ref,
    bg_lane_ref,
    grad_ref,
):
    rows, cells, _ = path_ref.shape
    pairs = every_ref.shape[0]
    blocks = 2 * pairs
    count = slope_sum_ref.shape[0]
    per = 128 // blocks
    together = grad_ref.shape[0]
    me = lax.axis_index("rx")

    for row in range(count + 2):
        for parity in range(2):
            place = parity * count + row if row < count else count + parity * 2 + row
            source = every_ref[:, place // 4, place % 4, :]
            all_ref[row, pl.ds(parity, pairs, stride=2), :] = source
    coherent = all_ref[count]
    power = all_ref[count + 1]
    scale_n, scale_d = patch_scales(total_tx, cot_ref, ids_ref[...] // PP, coherent, power)
    common = coherent * scale_n
    for t in range(count):
        bg_ref[t] = common + all_ref[t] * scale_d
    for half in range(count // per):
        stack = [bg_ref[half * per + i] for i in range(per)]
        bg_lane_ref[:, half * 128 : (half + 1) * 128] = jnp.concatenate(stack, axis=0).T
    start = jnp.zeros((cells, PB), F32)
    for t in range(count):
        own = bg_ref[t, pl.ds(me, 1), :] * slope_sum_ref[t : t + 1, :]
        start = start + tx_path_ref[t].astype(F32) * own

    def receivers(step, acc):
        acc = list(acc)
        for i in range(together):
            r = step * together + i
            grad = None
            for half in range(count // per):
                lanes = slice(half * 128, (half + 1) * 128)
                term = slope_ref[r, :, lanes] * bg_lane_ref[:, lanes]
                grad = term if grad is None else grad + term
            grad = grad.T
            total = grad[0:blocks]
            for group in range(1, per):
                total = total + grad[group * blocks : (group + 1) * blocks]
            grad_ref[i] = total
            for k in range(blocks):
                paths = path_ref[r, :, k * PB : (k + 1) * PB].astype(F32)
                acc[k % 2] = acc[k % 2] + paths * grad_ref[i, k : k + 1, :]
        return tuple(acc)

    acc = lax.fori_loop(0, rows // together, receivers, (start, jnp.zeros_like(start)))
    row = jnp.sum((acc[0] + acc[1]).T, axis=0, keepdims=True)
    row = jnp.concatenate([row] * (PB // cells), axis=1)
    out_ref[...] = jnp.broadcast_to(row, out_ref.shape)


def params(megabytes):
    return pltpu.CompilerParams(vmem_limit_bytes=megabytes * 1024 * 1024)


def whole(shape):
    return pl.BlockSpec(shape, lambda *_: (0,) * len(shape))


def shaped(*shape):
    return jax.ShapeDtypeStruct(shape, F32)


def in_hbm(array):
    return pltpu.with_memory_space_constraint(array, pltpu.HBM)


def tx_delays(s_row, tx_paths, rx_size):
    tx_count, _, own_pixels = tx_paths.shape
    return pl.pallas_call(
        tx_delay_kernel,
        in_specs=[pl.BlockSpec(memory_space=pl.ANY)] * 2,
        out_shape=shaped(rx_size, tx_count, own_pixels),
        scratch_shapes=[
            pltpu.VMEM(s_row.shape, s_row.dtype),
            pltpu.VMEM(tx_paths.shape, tx_paths.dtype),
            pltpu.SemaphoreType.DMA((2,)),
        ],
        compiler_params=params(4),
        name="tx_delay",
    )(in_hbm(s_row), in_hbm(tx_paths))


def prepare(s_row, rx_paths, traces, tap_start):
    rx_count, cells, pixels = rx_paths.shape
    tx_count, _, samples = traces.shape
    blocks = pixels // PB
    rows = 8
    return pl.pallas_call(
        prepare_kernel,
        grid=(rx_count // rows,),
        in_specs=[
            whole((1, cells)),
            pl.BlockSpec((rows, cells, pixels), lambda i: (i, 0, 0)),
            whole((tx_count, rx_count, samples)),
            whole((tx_count, rx_count, blocks)),
        ],
        out_specs=[
            pl.BlockSpec((rows, PB, 128), lambda i: (i, 0, 0)),
            pl.BlockSpec((rows, W, tx_count * blocks), lambda i: (i, 0, 0)),
        ],
        out_shape=[shaped(rx_count, PB, 128), shaped(rx_count, W, tx_count * blocks)],
        scratch_shapes=[
            pltpu.VMEM((tx_count, rx_count, samples), F32),
            pltpu.VMEM((rows, blocks, PB), F32),
        ],
        compiler_params=params(12),
        name="prepare",
    )(in_hbm(s_row), in_hbm(rx_paths), in_hbm(traces), in_hbm(tap_start))


def focus(tx_delay, rx_delay, window, rx_paths):
    blocks, tx_count, _ = tx_delay.shape
    rx_count = rx_delay.shape[0]
    lanes = tx_count * blocks
    vmem = pl.BlockSpec(memory_space=pltpu.VMEM)
    return pl.pallas_call(
        focus_kernel,
        in_specs=[vmem, vmem, vmem, pl.BlockSpec(memory_space=pl.ANY)],
        out_specs=[vmem] * 4,
        out_shape=[
            shaped(rx_count, PB, lanes),
            shaped(blocks // 2, 2 * tx_count, PB),
            shaped(blocks // 2, 2 * tx_count, PB),
            jax.ShapeDtypeStruct(rx_paths.shape, rx_paths.dtype),
        ],
        scratch_shapes=[pltpu.VMEM((PB, lanes), F32)] * 3
        + [pltpu.VMEM((128, PB), F32), pltpu.SemaphoreType.DMA],
        compiler_params=params(20),
        name="focus",
    )(tx_delay, rx_delay, window, in_hbm(rx_paths))


def gradient(total_tx, parts, patch_cotangent, every, pixel_order, slope_sum, tx_paths, slope, rx_paths):
    rx_count = rx_paths.shape[0]
    blocks = 2 * every.shape[0]
    tx_count = tx_paths.shape[0]
    lanes = tx_count * blocks
    together = 8
    vmem = pl.BlockSpec(memory_space=pltpu.VMEM)
    return pl.pallas_call(
        lambda *refs: gradient_kernel(total_tx, *refs),
        in_specs=[pl.BlockSpec(memory_space=pltpu.SMEM)] + [vmem] * 6,
        out_specs=vmem,
        out_shape=shaped(parts, PB),
        scratch_shapes=[
            pltpu.VMEM((tx_count + 2, blocks, PB), F32),
            pltpu.VMEM((tx_count, blocks, PB), F32),
            pltpu.VMEM((PB, lanes), F32),
            pltpu.VMEM((together, blocks, PB), F32),
        ],
        compiler_params=params(20),
        name="gradient",
    )(
        patch_cotangent,
        every,
        pixel_order.reshape(blocks, PB),
        slope_sum,
        tx_paths,
        slope,
        rx_paths,
    )


def on_device(slowness, tx_paths, rx_paths, traces, tap_start, pixel_order, patch_cotangent):
    tx_count, cells, _ = tx_paths.shape
    tx_size = lax.axis_size("tx")
    rx_size = lax.axis_size("rx")
    pairs = rx_size // 2
    s_row = slowness.reshape(1, cells)
    partner = [(i, i ^ 1) for i in range(rx_size)]
    same_core = [list(range(core, rx_size, 2)) for core in range(2)]

    def between_chips(array):
        return lax.all_to_all(array, "rx", 0, 0, axis_index_groups=same_core)

    delay = tx_delays(s_row, tx_paths, rx_size)
    rx_delay, window = prepare(s_row, rx_paths, traces, tap_start)
    tx_delay = lax.all_to_all(delay, "rx", 0, 0)
    slope, keep, give, path_copy = focus(tx_delay, rx_delay, window, rx_paths)
    got = lax.ppermute(give, "rx", partner)
    part = pl.pallas_call(
        pair_sum_kernel,
        out_shape=shaped(*keep.shape),
        compiler_params=params(4),
        name="sum_cores",
    )(keep, got)
    part = between_chips(part)
    beam, slope_sum = pl.pallas_call(
        gather_sum_kernel,
        out_shape=[shaped(tx_count, PB), shaped(tx_count, PB)],
        compiler_params=params(4),
        name="sum_receivers",
    )(part)
    other = lax.ppermute(beam, "rx", partner)
    pair = pl.pallas_call(
        square_kernel,
        out_shape=shaped(tx_size, 4, PB),
        compiler_params=params(4),
        name="squares",
    )(beam, other)
    pair = lax.all_to_all(pair, "tx", 0, 0)
    spread = pl.pallas_call(
        spread_kernel,
        out_shape=shaped(pairs, (2 * tx_count + 4) // 4, 4, PB),
        compiler_params=params(4),
        name="sum_transmits",
    )(pair, beam, other)
    every = between_chips(spread)
    share = gradient(
        tx_count * tx_size,
        tx_size * rx_size,
        patch_cotangent,
        every,
        pixel_order,
        slope_sum,
        tx_paths,
        slope,
        path_copy,
    )
    share = lax.all_to_all(share, ("tx", "rx"), 0, 0, tiled=True)
    return pl.pallas_call(
        total_kernel,
        out_shape=shaped(cells),
        compiler_params=params(4),
        name="total",
    )(share)


def solution(mesh):
    in_specs = (
        P(),
        P("tx", None, "rx"),
        P("rx", None, None),
        P("tx", "rx", None),
        P("tx", "rx", None),
        P(),
        P(),
    )
    out_specs = P()
    return jax.shard_map(
        on_device, mesh=mesh, in_specs=in_specs, out_specs=out_specs, check_vma=False
    )
```

```python
import math

import jax
import jax.numpy as jnp
from jax import lax
from jax.experimental import pallas as pl
from jax.experimental.pallas import tpu as pltpu
from jax.sharding import Mesh
from jax.sharding import PartitionSpec as P

W = 8
PB = 128
PP = 256
EPS = 1e-06
LN2 = math.log(2.0)
HALF_LOG2E = 0.5 / LN2
F32 = jnp.float32
FINE = (("zh", 2), ("y", 4), ("x", 4), ("zl", 4), ("c", 2))
TX = ("zh", "y")
RX = ("x", "zl", "c")


def block_diagonal(s_row, rows, cells):
    wide = jnp.concatenate([s_row] * rows, axis=1)
    shape = (rows, rows * cells)
    owner = lax.broadcasted_iota(jnp.int32, shape, 1) // cells
    mine = owner == lax.broadcasted_iota(jnp.int32, shape, 0)
    return jnp.where(mine, jnp.broadcast_to(wide, shape), 0.0).astype(jnp.bfloat16)


def tx_delay_kernel(s_hbm, path_hbm, out_ref, s_ref, path_ref, copied):
    fetches = [
        pltpu.make_async_copy(s_hbm, s_ref, copied.at[0]),
        pltpu.make_async_copy(path_hbm, path_ref, copied.at[1]),
    ]
    for fetch in fetches:
        fetch.start()
    for fetch in fetches:
        fetch.wait()
    rows, cells, width = path_ref.shape
    left = block_diagonal(s_ref[...].astype(F32), rows, cells)
    delay = jnp.dot(
        left, path_ref[...].reshape(rows * cells, width), preferred_element_type=F32
    )
    out_ref[...] = jnp.broadcast_to((delay * HALF_LOG2E)[None], out_ref.shape)


def prepare_kernel(s_ref, path_ref, trace_ref, start_ref, delay_ref, win_ref, sample_ref, plain_ref):
    step = pl.program_id(0)
    rows, cells, pixels = path_ref.shape
    count = trace_ref.shape[0]
    blocks = start_ref.shape[2]
    per = 128 // blocks

    @pl.when(step == 0)
    def _():
        sample_ref[...] = trace_ref[...].astype(F32)

    left = block_diagonal(s_ref[...].astype(F32), rows, cells)
    delay = jnp.dot(
        left, path_ref[...].reshape(rows * cells, pixels), preferred_element_type=F32
    )
    delay = delay * HALF_LOG2E
    for k in range(blocks):
        plain_ref[:, k, :] = delay[:, k * PB : (k + 1) * PB]
    for r in range(rows):
        delay_ref[r] = jnp.concatenate([plain_ref[r]] * per, axis=0).T

    mine = pl.ds(pl.multiple_of(step * rows, rows), rows)
    shape = (rows, 128)
    group = lax.broadcasted_iota(jnp.int32, shape, 1) // blocks
    for early in range(0, count, per):
        picks = []
        for t in range(early, early + per):
            starts = jnp.concatenate([start_ref[t, mine, :]] * per, axis=1)
            for first in range(0, W, per):
                index = starts + (group + first)
                low = index & 127
                high = index >> 7
                picked = None
                for part in range(sample_ref.shape[2] // 128):
                    source = sample_ref[t, mine, part * 128 : (part + 1) * 128]
                    got = jnp.take_along_axis(source, low, axis=1, mode="promise_in_bounds")
                    picked = got if picked is None else jnp.where(high == part, got, picked)
                picks.append(picked)
        for j in range(W):
            total = None
            for i in range(per):
                rolled = picks[i * (W // per) + j // per]
                shift = ((i - j % per) * blocks) % 128
                if shift:
                    rolled = pltpu.roll(rolled, shift, 1)
                total = rolled if total is None else jnp.where(group == i, rolled, total)
            off = j - (W - 1) / 2.0
            lanes = slice(early * blocks, early * blocks + 128)
            win_ref[:, j, lanes] = total * math.exp(-0.5 * off * off)


def focus_kernel(
    tx_ref,
    rx_ref,
    win_ref,
    path_ref,
    slope_ref,
    keep_ref,
    give_ref,
    path_copy_ref,
    tx_lane_ref,
    total_f_ref,
    total_s_ref,
    turned_ref,
    copied,
):
    fetch = pltpu.make_async_copy(path_ref, path_copy_ref, copied)
    fetch.start()
    blocks, count, _ = tx_ref.shape
    rows = rx_ref.shape[0]
    per = 128 // blocks
    limit = 9.25 / LN2
    halves = count // per

    for half in range(halves):
        stack = [tx_ref[:, half * per + i, :] for i in range(per)]
        tx_lane_ref[:, half * 128 : (half + 1) * 128] = jnp.concatenate(stack, axis=0).T
    total_f_ref[...] = jnp.zeros_like(total_f_ref)
    total_s_ref[...] = jnp.zeros_like(total_s_ref)

    def horner(z, c3, c2, c1, c0):
        p1 = c3 * z + c2
        p2 = p1 * z + c1
        d2 = c3 * z + p1
        return p2 * z + c0, d2 * z + p2

    def point(tap, h):
        h = jnp.minimum(jnp.maximum(h, -limit), limit)
        m = h * (-LN2)
        s = jnp.exp2(h)
        si = jnp.exp2(-h)
        gauss = jnp.exp2(m * h)
        u = s * s
        v = si * si
        up, dup = horner(u, tap[7], tap[6], tap[5], tap[4])
        down, ddown = horner(v, tap[0], tap[1], tap[2], tap[3])
        x = s * up
        y = si * down
        both = x + y
        change = (x - y) * 0.5 + ((s * u) * dup - (si * v) * ddown)
        focused = gauss * (gauss * both)
        slope = gauss * (gauss * (change + (m + m) * both))
        return focused, slope

    def receivers(step, carry):
        for half in range(halves):
            lanes = slice(half * 128, (half + 1) * 128)
            taps = [
                [
                    jnp.broadcast_to(win_ref[2 * step + i, j : j + 1, lanes], (8, 128))
                    for j in range(W)
                ]
                for i in range(2)
            ]
            for first in range(0, PB, 8):
                here = slice(first, first + 8)
                total_f = total_f_ref[here, lanes]
                total_s = total_s_ref[here, lanes]
                for i in range(2):
                    h = tx_lane_ref[here, lanes] + rx_ref[2 * step + i, here, :]
                    focused, slope = point(taps[i], h)
                    slope_ref[2 * step + i, here, lanes] = slope
                    total_f = total_f + focused
                    total_s = total_s + slope
                total_f_ref[here, lanes] = total_f
                total_s_ref[here, lanes] = total_s
        return carry

    lax.fori_loop(0, rows // 2, receivers, 0)
    mine = lax.axis_index("c")
    for source, base in ((total_f_ref, 0), (total_s_ref, count)):
        for half in range(halves):
            turned_ref[...] = source[:, half * 128 : (half + 1) * 128].T
            for i in range(per):
                row = base + half * per + i
                even = turned_ref[pl.ds(i * blocks, blocks // 2, stride=2), :]
                odd = turned_ref[pl.ds(i * blocks + 1, blocks // 2, stride=2), :]
                keep_ref[:, row, :] = jnp.where(mine == 0, even, odd)
                give_ref[:, row, :] = jnp.where(mine == 0, odd, even)
    fetch.wait()


def pair_sum_kernel(keep_ref, got_ref, out_ref):
    out_ref[...] = keep_ref[...] + got_ref[...]


def sum_x_kernel(part_ref, out_ref):
    sources, blocks, rows, _ = part_ref.shape
    count = rows // 2
    for block in range(blocks):
        total = part_ref[0, block]
        for i in range(1, sources):
            total = total + part_ref[i, block]
        here = slice(block * count, (block + 1) * count)
        beam = total[0:count]
        out_ref[:, here] = jnp.broadcast_to(beam[None], (out_ref.shape[0], count, PB))
        for far in range(out_ref.shape[0] // blocks):
            out_ref[far * blocks + block, blocks * count :] = total[count:rows]


def sum_z_kernel(part_ref, out_ref, slope_sum_ref):
    blocks = 4
    rows = part_ref.shape[1]
    count = rows // (blocks + 1)
    first = lax.axis_index("zh") == 0
    totals = []
    for far in range(part_ref.shape[0] // blocks):
        total = part_ref[far * blocks]
        for i in range(1, blocks):
            total = total + part_ref[far * blocks + i]
        totals.append(total)
    own = jnp.where(first, totals[0], totals[1])
    slope_sum_ref[...] = own[blocks * count :]
    lines = []
    for power in (False, True):
        for block in range(blocks):
            line = None
            for total in totals:
                beam = total[block * count : (block + 1) * count]
                part = jnp.sum(beam * beam if power else beam, axis=0, keepdims=True)
                line = part if line is None else line + part
            lines.append(line)
    wide = out_ref.shape[0]
    out_ref[:, 0 : blocks * count] = jnp.broadcast_to(
        own[0 : blocks * count][None], (wide, blocks * count, PB)
    )
    out_ref[:, blocks * count :] = jnp.broadcast_to(
        jnp.concatenate(lines, axis=0)[None], (wide, 2 * blocks, PB)
    )


def sum_y_kernel(part_ref, out_ref):
    own = lax.axis_index("y")
    sides = 4
    blocks = 4
    count = out_ref.shape[1] - 2
    for x in range(part_ref.shape[0] // sides):
        total = part_ref[x * sides, blocks * count :, :]
        for y in range(1, sides):
            total = total + part_ref[x * sides + y, blocks * count :, :]
        beams = part_ref[x * sides + own, 0 : blocks * count, :]
        for block in range(blocks):
            place = x * blocks + block
            out_ref[place, 0:count] = beams[block * count : (block + 1) * count]
            out_ref[place, count : count + 1] = total[block : block + 1]
            out_ref[place, count + 1 : count + 2] = total[blocks + block : blocks + block + 1]


def total_kernel(share_ref, out_ref):
    out_ref[...] = jnp.sum(share_ref[...], axis=0)[0 : out_ref.shape[0]]


def patch_scales(total_tx, cot_ref, ids, coherent, power):
    patches = cot_ref.shape[0]
    square = coherent * coherent
    sums = []
    for field in (square, power):
        rows = [
            jnp.sum(jnp.where(ids == q, field, 0.0), axis=0, keepdims=True)
            for q in range(patches)
        ]
        sums.append(jnp.sum(jnp.concatenate(rows, axis=0), axis=1, keepdims=True))
    numer, power_sum = sums
    denom = total_tx * power_sum
    cot = jnp.zeros_like(numer)
    row = lax.broadcasted_iota(jnp.int32, cot.shape, 0)
    for q in range(patches):
        cot = jnp.where(row == q, cot_ref[q], cot)
    value_n = -2.0 * (cot / (numer + EPS))
    value_d = 2.0 * (cot * total_tx / (denom + EPS))
    scale_n = jnp.zeros_like(square)
    scale_d = jnp.zeros_like(square)
    for q in range(patches):
        inside = ids == q
        scale_n = jnp.where(inside, value_n[q : q + 1, :], scale_n)
        scale_d = jnp.where(inside, value_d[q : q + 1, :], scale_d)
    return scale_n, scale_d


def gradient_kernel(
    total_tx,
    cot_ref,
    here_ref,
    there_ref,
    ids_ref,
    slope_sum_ref,
    tx_path_ref,
    slope_ref,
    path_ref,
    out_ref,
    all_ref,
    bg_ref,
    bg_lane_ref,
    grad_ref,
):
    rows, cells, _ = path_ref.shape
    pairs = here_ref.shape[0]
    blocks = 2 * pairs
    count = slope_sum_ref.shape[0]
    per = 128 // blocks
    together = grad_ref.shape[0]
    core = lax.axis_index("c")
    me = (lax.axis_index("x") * lax.axis_size("zl") + lax.axis_index("zl")) * 2 + core

    for row in range(count + 2):
        here = here_ref[:, row, :]
        there = there_ref[:, row, :]
        all_ref[row, pl.ds(0, pairs, stride=2), :] = jnp.where(core == 0, here, there)
        all_ref[row, pl.ds(1, pairs, stride=2), :] = jnp.where(core == 0, there, here)
    coherent = all_ref[count]
    power = all_ref[count + 1]
    scale_n, scale_d = patch_scales(total_tx, cot_ref, ids_ref[...] // PP, coherent, power)
    common = coherent * scale_n
    for t in range(count):
        bg_ref[t] = common + all_ref[t] * scale_d
    for half in range(count // per):
        stack = [bg_ref[half * per + i] for i in range(per)]
        bg_lane_ref[:, half * 128 : (half + 1) * 128] = jnp.concatenate(stack, axis=0).T
    start = jnp.zeros((cells, PB), F32)
    for t in range(count):
        own = bg_ref[t, pl.ds(me, 1), :] * slope_sum_ref[t : t + 1, :]
        start = start + tx_path_ref[t].astype(F32) * own

    def receivers(step, acc):
        acc = list(acc)
        for i in range(together):
            r = step * together + i
            grad = None
            for half in range(count // per):
                lanes = slice(half * 128, (half + 1) * 128)
                term = slope_ref[r, :, lanes] * bg_lane_ref[:, lanes]
                grad = term if grad is None else grad + term
            grad = grad.T
            total = grad[0:blocks]
            for group in range(1, per):
                total = total + grad[group * blocks : (group + 1) * blocks]
            grad_ref[i] = total
            for k in range(blocks):
                paths = path_ref[r, :, k * PB : (k + 1) * PB].astype(F32)
                acc[k % 2] = acc[k % 2] + paths * grad_ref[i, k : k + 1, :]
        return tuple(acc)

    acc = lax.fori_loop(0, rows // together, receivers, (start, jnp.zeros_like(start)))
    row = jnp.sum((acc[0] + acc[1]).T, axis=0, keepdims=True)
    row = jnp.concatenate([row] * (PB // cells), axis=1)
    out_ref[...] = jnp.broadcast_to(row, out_ref.shape)


def params(megabytes):
    return pltpu.CompilerParams(vmem_limit_bytes=megabytes * 1024 * 1024)


def whole(shape):
    return pl.BlockSpec(shape, lambda *_: (0,) * len(shape))


def shaped(*shape):
    return jax.ShapeDtypeStruct(shape, F32)


def in_hbm(array):
    return pltpu.with_memory_space_constraint(array, pltpu.HBM)


def tx_delays(s_row, tx_paths, rx_size):
    tx_count, _, own_pixels = tx_paths.shape
    return pl.pallas_call(
        tx_delay_kernel,
        in_specs=[pl.BlockSpec(memory_space=pl.ANY)] * 2,
        out_shape=shaped(rx_size, tx_count, own_pixels),
        scratch_shapes=[
            pltpu.VMEM(s_row.shape, s_row.dtype),
            pltpu.VMEM(tx_paths.shape, tx_paths.dtype),
            pltpu.SemaphoreType.DMA((2,)),
        ],
        compiler_params=params(4),
        name="tx_delay",
    )(in_hbm(s_row), in_hbm(tx_paths))


def prepare(s_row, rx_paths, traces, tap_start):
    rx_count, cells, pixels = rx_paths.shape
    tx_count, _, samples = traces.shape
    blocks = pixels // PB
    rows = 8
    return pl.pallas_call(
        prepare_kernel,
        grid=(rx_count // rows,),
        in_specs=[
            whole((1, cells)),
            pl.BlockSpec((rows, cells, pixels), lambda i: (i, 0, 0)),
            whole((tx_count, rx_count, samples)),
            whole((tx_count, rx_count, blocks)),
        ],
        out_specs=[
            pl.BlockSpec((rows, PB, 128), lambda i: (i, 0, 0)),
            pl.BlockSpec((rows, W, tx_count * blocks), lambda i: (i, 0, 0)),
        ],
        out_shape=[shaped(rx_count, PB, 128), shaped(rx_count, W, tx_count * blocks)],
        scratch_shapes=[
            pltpu.VMEM((tx_count, rx_count, samples), F32),
            pltpu.VMEM((rows, blocks, PB), F32),
        ],
        compiler_params=params(12),
        name="prepare",
    )(in_hbm(s_row), in_hbm(rx_paths), in_hbm(traces), in_hbm(tap_start))


def focus(tx_delay, rx_delay, window, rx_paths):
    blocks, tx_count, _ = tx_delay.shape
    rx_count = rx_delay.shape[0]
    lanes = tx_count * blocks
    vmem = pl.BlockSpec(memory_space=pltpu.VMEM)
    return pl.pallas_call(
        focus_kernel,
        in_specs=[vmem, vmem, vmem, pl.BlockSpec(memory_space=pl.ANY)],
        out_specs=[vmem] * 4,
        out_shape=[
            shaped(rx_count, PB, lanes),
            shaped(blocks // 2, 2 * tx_count, PB),
            shaped(blocks // 2, 2 * tx_count, PB),
            jax.ShapeDtypeStruct(rx_paths.shape, rx_paths.dtype),
        ],
        scratch_shapes=[pltpu.VMEM((PB, lanes), F32)] * 3
        + [pltpu.VMEM((128, PB), F32), pltpu.SemaphoreType.DMA],
        compiler_params=params(20),
        name="focus",
    )(tx_delay, rx_delay, window, in_hbm(rx_paths))


def gradient(total_tx, parts, patch_cotangent, here, there, pixel_order, slope_sum, tx_paths, slope, rx_paths):
    rx_count = rx_paths.shape[0]
    blocks = 2 * here.shape[0]
    tx_count = tx_paths.shape[0]
    lanes = tx_count * blocks
    together = 8
    vmem = pl.BlockSpec(memory_space=pltpu.VMEM)
    return pl.pallas_call(
        lambda *refs: gradient_kernel(total_tx, *refs),
        in_specs=[pl.BlockSpec(memory_space=pltpu.SMEM)] + [vmem] * 7,
        out_specs=vmem,
        out_shape=shaped(parts, PB),
        scratch_shapes=[
            pltpu.VMEM((tx_count + 2, blocks, PB), F32),
            pltpu.VMEM((tx_count, blocks, PB), F32),
            pltpu.VMEM((PB, lanes), F32),
            pltpu.VMEM((together, blocks, PB), F32),
        ],
        compiler_params=params(20),
        name="gradient",
    )(
        patch_cotangent,
        here,
        there,
        pixel_order.reshape(blocks, PB),
        slope_sum,
        tx_paths,
        slope,
        rx_paths,
    )


def local(kernel, name, out_shape, *arrays):
    return pl.pallas_call(
        kernel, out_shape=out_shape, compiler_params=params(4), name=name
    )(*arrays)


def on_device(slowness, tx_paths, rx_paths, traces, tap_start, pixel_order, patch_cotangent):
    tx_count, cells, _ = tx_paths.shape
    rx_size = lax.axis_size(RX)
    tx_size = lax.axis_size(TX)
    x_size = lax.axis_size("x")
    near = lax.axis_size("zl")
    pairs = x_size * near
    s_row = slowness.reshape(1, cells)
    swap = [(0, 1), (1, 0)]

    delay = tx_delays(s_row, tx_paths, rx_size)
    rx_delay, window = prepare(s_row, rx_paths, traces, tap_start)
    tx_delay = lax.all_to_all(delay, RX, 0, 0)
    slope, keep, give, path_copy = focus(tx_delay, rx_delay, window, rx_paths)
    got = lax.ppermute(give, "c", swap)
    part = local(pair_sum_kernel, "sum_cores", shaped(*keep.shape), keep, got)
    part = lax.all_to_all(part.reshape(x_size, near, 2 * tx_count, PB), "x", 0, 0)
    rows = (near + 1) * tx_count
    part = local(sum_x_kernel, "sum_x", shaped(2 * near, rows, PB), part)
    part = lax.all_to_all(part, ("zh", "zl"), 0, 0)
    rows = near * (tx_count + 2)
    part, slope_sum = local(
        sum_z_kernel,
        "sum_z",
        [shaped(x_size * lax.axis_size("y"), rows, PB), shaped(tx_count, PB)],
        part,
    )
    part = lax.all_to_all(part, ("x", "y"), 0, 0)
    here = local(sum_y_kernel, "sum_y", shaped(pairs, tx_count + 2, PB), part)
    there = lax.ppermute(here, "c", swap)
    share = gradient(
        tx_count * tx_size,
        tx_size * rx_size,
        patch_cotangent,
        here,
        there,
        pixel_order,
        slope_sum,
        tx_paths,
        slope,
        path_copy,
    )
    share = lax.all_to_all(share, TX + RX, 0, 0, tiled=True)
    return local(total_kernel, "total", shaped(cells), share)


def solution(mesh):
    names = tuple(name for name, _ in FINE)
    fine = Mesh(mesh.devices.reshape([size for _, size in FINE]), names)
    in_specs = (
        P(),
        P(TX, None, RX),
        P(RX, None, None),
        P(TX, RX, None),
        P(TX, RX, None),
        P(),
        P(),
    )
    out_specs = P()
    return jax.shard_map(
        on_device, mesh=fine, in_specs=in_specs, out_specs=out_specs, check_vma=False
    )
```

```python
import math

import jax
import jax.numpy as jnp
from jax import lax
from jax.experimental import pallas as pl
from jax.experimental.pallas import tpu as pltpu
from jax.sharding import Mesh
from jax.sharding import PartitionSpec as P

W = 8
PB = 128
PP = 256
EPS = 1e-06
LN2 = math.log(2.0)
LOG2E = 1.0 / LN2
F32 = jnp.float32
FINE = (("zh", 2), ("y", 4), ("x", 4), ("zl", 4), ("c", 2))
TX = ("zh", "y")
RX = ("x", "zl", "c")


def block_diagonal(s_row, rows, cells):
    wide = jnp.concatenate([s_row] * rows, axis=1)
    shape = (rows, rows * cells)
    owner = lax.broadcasted_iota(jnp.int32, shape, 1) // cells
    mine = owner == lax.broadcasted_iota(jnp.int32, shape, 0)
    return jnp.where(mine, jnp.broadcast_to(wide, shape), 0.0).astype(jnp.bfloat16)


def tx_delay_kernel(s_hbm, path_hbm, out_ref, s_ref, path_ref, copied):
    fetches = [
        pltpu.make_async_copy(s_hbm, s_ref, copied.at[0]),
        pltpu.make_async_copy(path_hbm, path_ref, copied.at[1]),
    ]
    for fetch in fetches:
        fetch.start()
    for fetch in fetches:
        fetch.wait()
    rows, cells, width = path_ref.shape
    left = block_diagonal(s_ref[...].astype(F32), rows, cells)
    delay = jnp.dot(
        left, path_ref[...].reshape(rows * cells, width), preferred_element_type=F32
    )
    out_ref[...] = jnp.broadcast_to((delay * -LOG2E)[None], out_ref.shape)


def prepare_kernel(
    s_hbm,
    path_hbm,
    trace_hbm,
    start_hbm,
    delay_ref,
    win_ref,
    s_ref,
    path_ref,
    trace_ref,
    start_ref,
    sample_ref,
    plain_ref,
    copied,
):
    rx_count, cells, pixels = path_ref.shape
    count = trace_ref.shape[0]
    blocks = start_ref.shape[2]
    per = 128 // blocks
    rows = plain_ref.shape[0]
    groups = rx_count // rows

    fetches = [
        pltpu.make_async_copy(trace_hbm, trace_ref, copied.at[0]),
        pltpu.make_async_copy(start_hbm, start_ref, copied.at[1]),
        pltpu.make_async_copy(s_hbm, s_ref, copied.at[2]),
    ]
    for i in range(groups):
        some = pl.ds(i * rows, rows)
        fetches.append(
            pltpu.make_async_copy(path_hbm.at[some], path_ref.at[some], copied.at[3 + i])
        )
    for fetch in fetches:
        fetch.start()
    for fetch in fetches[:3]:
        fetch.wait()

    sample_ref[...] = trace_ref[...].astype(F32)
    lane_group = lax.broadcasted_iota(jnp.int32, (rows, 128), 1) // blocks

    def windows(step, carry):
        mine = pl.ds(pl.multiple_of(step * rows, rows), rows)
        for early in range(0, count, per):
            picks = []
            for t in range(early, early + per):
                starts = jnp.concatenate([start_ref[t, mine, :]] * per, axis=1)
                for first in range(0, W, per):
                    index = starts + (lane_group + first)
                    low = index & 127
                    high = index >> 7
                    picked = None
                    for part in range(sample_ref.shape[2] // 128):
                        source = sample_ref[t, mine, part * 128 : (part + 1) * 128]
                        got = jnp.take_along_axis(
                            source, low, axis=1, mode="promise_in_bounds"
                        )
                        picked = got if picked is None else jnp.where(high == part, got, picked)
                    picks.append(picked)
            lanes = slice(early * blocks, early * blocks + 128)
            for j in range(W):
                total = None
                for i in range(per):
                    rolled = picks[i * (W // per) + j // per]
                    shift = ((i - j % per) * blocks) % 128
                    if shift:
                        rolled = pltpu.roll(rolled, shift, 1)
                    total = rolled if total is None else jnp.where(lane_group == i, rolled, total)
                win_ref[mine, j, lanes] = total * math.exp(-0.5 * j * j)
        return carry

    lax.fori_loop(0, groups, windows, 0)
    left = block_diagonal(s_ref[...].astype(F32), rows, cells)
    for i in range(groups):
        fetches[3 + i].wait()
        paths = path_ref[i * rows : (i + 1) * rows].reshape(rows * cells, pixels)
        delay = jnp.dot(left, paths, preferred_element_type=F32)
        delay = delay * -LOG2E - (W - 1) / 2.0 * LOG2E
        for k in range(blocks):
            plain_ref[:, k, :] = delay[:, k * PB : (k + 1) * PB]
        for r in range(rows):
            delay_ref[i * rows + r] = jnp.concatenate([plain_ref[r]] * per, axis=0).T


def focus_kernel(
    tx_ref,
    rx_ref,
    win_ref,
    path_ref,
    slope_ref,
    keep_ref,
    give_ref,
    path_copy_ref,
    tx_lane_ref,
    total_f_ref,
    total_s_ref,
    turned_ref,
    copied,
):
    fetch = pltpu.make_async_copy(path_ref, path_copy_ref, copied)
    fetch.start()
    blocks, count, _ = tx_ref.shape
    rows = rx_ref.shape[0]
    per = 128 // blocks
    halves = count // per

    for half in range(halves):
        stack = [tx_ref[:, half * per + i, :] for i in range(per)]
        tx_lane_ref[:, half * 128 : (half + 1) * 128] = jnp.concatenate(stack, axis=0).T
    total_f_ref[...] = jnp.zeros_like(total_f_ref)
    total_s_ref[...] = jnp.zeros_like(total_s_ref)

    def point(tap, tau):
        ratio = jnp.exp2(tau)
        twice = tau + tau
        power = tau * (tau * (-0.5 * LN2) - (W - 1.0))
        focused = None
        for j in range(W - 1, -1, -2):
            upper = jnp.exp2(power)
            lower = upper * ratio
            if focused is None:
                focused = tap[j] * upper
                moment = focused
            else:
                focused = focused + tap[j] * upper
                moment = moment + focused
            focused = focused + tap[j - 1] * lower
            if j > 1:
                moment = moment + focused
                power = power + twice
        return focused, moment * LOG2E + tau * focused

    def receivers(step, carry):
        for half in range(halves):
            lanes = slice(half * 128, (half + 1) * 128)
            taps = [
                [
                    jnp.broadcast_to(win_ref[2 * step + i, j : j + 1, lanes], (8, 128))
                    for j in range(W)
                ]
                for i in range(2)
            ]
            for first in range(0, PB, 8):
                here = slice(first, first + 8)
                total_f = total_f_ref[here, lanes]
                total_s = total_s_ref[here, lanes]
                for i in range(2):
                    tau = tx_lane_ref[here, lanes] + rx_ref[2 * step + i, here, :]
                    focused, slope = point(taps[i], tau)
                    slope_ref[2 * step + i, here, lanes] = slope
                    total_f = total_f + focused
                    total_s = total_s + slope
                total_f_ref[here, lanes] = total_f
                total_s_ref[here, lanes] = total_s
        return carry

    lax.fori_loop(0, rows // 2, receivers, 0)
    mine = lax.axis_index("c")
    for source, base in ((total_f_ref, 0), (total_s_ref, count)):
        for half in range(halves):
            turned_ref[...] = source[:, half * 128 : (half + 1) * 128].T
            for i in range(per):
                row = base + half * per + i
                even = turned_ref[pl.ds(i * blocks, blocks // 2, stride=2), :]
                odd = turned_ref[pl.ds(i * blocks + 1, blocks // 2, stride=2), :]
                keep_ref[:, row, :] = jnp.where(mine == 0, even, odd)
                give_ref[:, row, :] = jnp.where(mine == 0, odd, even)
    fetch.wait()


def pair_sum_kernel(keep_ref, got_ref, out_ref):
    out_ref[...] = keep_ref[...] + got_ref[...]


def sum_x_kernel(part_ref, out_ref):
    sources, blocks, rows, _ = part_ref.shape
    count = rows // 2
    for block in range(blocks):
        total = part_ref[0, block]
        for i in range(1, sources):
            total = total + part_ref[i, block]
        here = slice(block * count, (block + 1) * count)
        beam = total[0:count]
        out_ref[:, here] = jnp.broadcast_to(beam[None], (out_ref.shape[0], count, PB))
        for far in range(out_ref.shape[0] // blocks):
            out_ref[far * blocks + block, blocks * count :] = total[count:rows]


def sum_z_kernel(part_ref, out_ref, slope_sum_ref):
    blocks = 4
    rows = part_ref.shape[1]
    count = rows // (blocks + 1)
    first = lax.axis_index("zh") == 0
    totals = []
    for far in range(part_ref.shape[0] // blocks):
        total = part_ref[far * blocks]
        for i in range(1, blocks):
            total = total + part_ref[far * blocks + i]
        totals.append(total)
    own = jnp.where(first, totals[0], totals[1])
    slope_sum_ref[...] = own[blocks * count :]
    lines = []
    for power in (False, True):
        for block in range(blocks):
            line = None
            for total in totals:
                beam = total[block * count : (block + 1) * count]
                part = jnp.sum(beam * beam if power else beam, axis=0, keepdims=True)
                line = part if line is None else line + part
            lines.append(line)
    wide = out_ref.shape[0]
    out_ref[:, 0 : blocks * count] = jnp.broadcast_to(
        own[0 : blocks * count][None], (wide, blocks * count, PB)
    )
    out_ref[:, blocks * count :] = jnp.broadcast_to(
        jnp.concatenate(lines, axis=0)[None], (wide, 2 * blocks, PB)
    )


def sum_y_kernel(part_ref, out_ref):
    own = lax.axis_index("y")
    sides = 4
    blocks = 4
    count = out_ref.shape[1] - 2
    for x in range(part_ref.shape[0] // sides):
        total = part_ref[x * sides, blocks * count :, :]
        for y in range(1, sides):
            total = total + part_ref[x * sides + y, blocks * count :, :]
        beams = part_ref[x * sides + own, 0 : blocks * count, :]
        for block in range(blocks):
            place = x * blocks + block
            out_ref[place, 0:count] = beams[block * count : (block + 1) * count]
            out_ref[place, count : count + 1] = total[block : block + 1]
            out_ref[place, count + 1 : count + 2] = total[blocks + block : blocks + block + 1]


def total_kernel(share_ref, out_ref):
    out_ref[...] = jnp.sum(share_ref[...], axis=0)[0 : out_ref.shape[0]]


def patch_scales(total_tx, cot_ref, ids, coherent, power):
    patches = cot_ref.shape[0]
    square = coherent * coherent
    sums = []
    for field in (square, power):
        rows = [
            jnp.sum(jnp.where(ids == q, field, 0.0), axis=0, keepdims=True)
            for q in range(patches)
        ]
        sums.append(jnp.sum(jnp.concatenate(rows, axis=0), axis=1, keepdims=True))
    numer, power_sum = sums
    denom = total_tx * power_sum
    cot = jnp.zeros_like(numer)
    row = lax.broadcasted_iota(jnp.int32, cot.shape, 0)
    for q in range(patches):
        cot = jnp.where(row == q, cot_ref[q], cot)
    value_n = -2.0 * (cot / (numer + EPS))
    value_d = 2.0 * (cot * total_tx / (denom + EPS))
    scale_n = jnp.zeros_like(square)
    scale_d = jnp.zeros_like(square)
    for q in range(patches):
        inside = ids == q
        scale_n = jnp.where(inside, value_n[q : q + 1, :], scale_n)
        scale_d = jnp.where(inside, value_d[q : q + 1, :], scale_d)
    return scale_n, scale_d


def gradient_kernel(
    total_tx,
    cot_ref,
    here_ref,
    there_ref,
    ids_ref,
    slope_sum_ref,
    tx_path_ref,
    slope_ref,
    path_ref,
    out_ref,
    all_ref,
    bg_ref,
    bg_lane_ref,
    grad_ref,
):
    rows, cells, _ = path_ref.shape
    pairs = here_ref.shape[0]
    blocks = 2 * pairs
    count = slope_sum_ref.shape[0]
    per = 128 // blocks
    together = grad_ref.shape[0]
    core = lax.axis_index("c")
    me = (lax.axis_index("x") * lax.axis_size("zl") + lax.axis_index("zl")) * 2 + core

    for row in range(count + 2):
        here = here_ref[:, row, :]
        there = there_ref[:, row, :]
        all_ref[row, pl.ds(0, pairs, stride=2), :] = jnp.where(core == 0, here, there)
        all_ref[row, pl.ds(1, pairs, stride=2), :] = jnp.where(core == 0, there, here)
    coherent = all_ref[count]
    power = all_ref[count + 1]
    scale_n, scale_d = patch_scales(total_tx, cot_ref, ids_ref[...] // PP, coherent, power)
    common = coherent * scale_n
    for t in range(count):
        bg_ref[t] = common + all_ref[t] * scale_d
    for half in range(count // per):
        stack = [bg_ref[half * per + i] for i in range(per)]
        bg_lane_ref[:, half * 128 : (half + 1) * 128] = jnp.concatenate(stack, axis=0).T
    start = jnp.zeros((cells, PB), F32)
    for t in range(count):
        own = bg_ref[t, pl.ds(me, 1), :] * slope_sum_ref[t : t + 1, :]
        start = start + tx_path_ref[t].astype(F32) * own

    def receivers(step, acc):
        acc = list(acc)
        for i in range(together):
            r = step * together + i
            grad = None
            for half in range(count // per):
                lanes = slice(half * 128, (half + 1) * 128)
                term = slope_ref[r, :, lanes] * bg_lane_ref[:, lanes]
                grad = term if grad is None else grad + term
            grad = grad.T
            total = grad[0:blocks]
            for group in range(1, per):
                total = total + grad[group * blocks : (group + 1) * blocks]
            grad_ref[i] = total
            for k in range(blocks):
                paths = path_ref[r, :, k * PB : (k + 1) * PB].astype(F32)
                acc[k % 2] = acc[k % 2] + paths * grad_ref[i, k : k + 1, :]
        return tuple(acc)

    acc = lax.fori_loop(0, rows // together, receivers, (start, jnp.zeros_like(start)))
    row = jnp.sum((acc[0] + acc[1]).T, axis=0, keepdims=True) * LN2
    row = jnp.concatenate([row] * (PB // cells), axis=1)
    out_ref[...] = jnp.broadcast_to(row, out_ref.shape)


def params(megabytes):
    return pltpu.CompilerParams(vmem_limit_bytes=megabytes * 1024 * 1024)


def whole(shape):
    return pl.BlockSpec(shape, lambda *_: (0,) * len(shape))


def shaped(*shape):
    return jax.ShapeDtypeStruct(shape, F32)


def in_hbm(array):
    return pltpu.with_memory_space_constraint(array, pltpu.HBM)


def tx_delays(s_row, tx_paths, rx_size):
    tx_count, _, own_pixels = tx_paths.shape
    return pl.pallas_call(
        tx_delay_kernel,
        in_specs=[pl.BlockSpec(memory_space=pl.ANY)] * 2,
        out_shape=shaped(rx_size, tx_count, own_pixels),
        scratch_shapes=[
            pltpu.VMEM(s_row.shape, s_row.dtype),
            pltpu.VMEM(tx_paths.shape, tx_paths.dtype),
            pltpu.SemaphoreType.DMA((2,)),
        ],
        compiler_params=params(4),
        name="tx_delay",
    )(in_hbm(s_row), in_hbm(tx_paths))


def prepare(s_row, rx_paths, traces, tap_start):
    rx_count, cells, pixels = rx_paths.shape
    tx_count, _, samples = traces.shape
    blocks = pixels // PB
    rows = 8
    vmem = pl.BlockSpec(memory_space=pltpu.VMEM)
    arrays = (s_row, rx_paths, traces, tap_start)
    return pl.pallas_call(
        prepare_kernel,
        in_specs=[pl.BlockSpec(memory_space=pl.ANY)] * len(arrays),
        out_specs=[vmem] * 2,
        out_shape=[shaped(rx_count, PB, 128), shaped(rx_count, W, tx_count * blocks)],
        scratch_shapes=[pltpu.VMEM(array.shape, array.dtype) for array in arrays]
        + [
            pltpu.VMEM((tx_count, rx_count, samples), F32),
            pltpu.VMEM((rows, blocks, PB), F32),
            pltpu.SemaphoreType.DMA((len(arrays) - 1 + rx_count // rows,)),
        ],
        compiler_params=params(20),
        name="prepare",
    )(*(in_hbm(array) for array in arrays))


def focus(tx_delay, rx_delay, window, rx_paths):
    blocks, tx_count, _ = tx_delay.shape
    rx_count = rx_delay.shape[0]
    lanes = tx_count * blocks
    vmem = pl.BlockSpec(memory_space=pltpu.VMEM)
    return pl.pallas_call(
        focus_kernel,
        in_specs=[vmem, vmem, vmem, pl.BlockSpec(memory_space=pl.ANY)],
        out_specs=[vmem] * 4,
        out_shape=[
            shaped(rx_count, PB, lanes),
            shaped(blocks // 2, 2 * tx_count, PB),
            shaped(blocks // 2, 2 * tx_count, PB),
            jax.ShapeDtypeStruct(rx_paths.shape, rx_paths.dtype),
        ],
        scratch_shapes=[pltpu.VMEM((PB, lanes), F32)] * 3
        + [pltpu.VMEM((128, PB), F32), pltpu.SemaphoreType.DMA],
        compiler_params=params(20),
        name="focus",
    )(tx_delay, rx_delay, window, in_hbm(rx_paths))


def gradient(total_tx, parts, patch_cotangent, here, there, pixel_order, slope_sum, tx_paths, slope, rx_paths):
    rx_count = rx_paths.shape[0]
    blocks = 2 * here.shape[0]
    tx_count = tx_paths.shape[0]
    lanes = tx_count * blocks
    together = 8
    vmem = pl.BlockSpec(memory_space=pltpu.VMEM)
    return pl.pallas_call(
        lambda *refs: gradient_kernel(total_tx, *refs),
        in_specs=[pl.BlockSpec(memory_space=pltpu.SMEM)] + [vmem] * 7,
        out_specs=vmem,
        out_shape=shaped(parts, PB),
        scratch_shapes=[
            pltpu.VMEM((tx_count + 2, blocks, PB), F32),
            pltpu.VMEM((tx_count, blocks, PB), F32),
            pltpu.VMEM((PB, lanes), F32),
            pltpu.VMEM((together, blocks, PB), F32),
        ],
        compiler_params=params(20),
        name="gradient",
    )(
        patch_cotangent,
        here,
        there,
        pixel_order.reshape(blocks, PB),
        slope_sum,
        tx_paths,
        slope,
        rx_paths,
    )


def local(kernel, name, out_shape, *arrays):
    return pl.pallas_call(
        kernel, out_shape=out_shape, compiler_params=params(4), name=name
    )(*arrays)


def on_device(slowness, tx_paths, rx_paths, traces, tap_start, pixel_order, patch_cotangent):
    tx_count, cells, _ = tx_paths.shape
    rx_size = lax.axis_size(RX)
    tx_size = lax.axis_size(TX)
    x_size = lax.axis_size("x")
    near = lax.axis_size("zl")
    pairs = x_size * near
    s_row = slowness.reshape(1, cells)
    swap = [(0, 1), (1, 0)]

    delay = tx_delays(s_row, tx_paths, rx_size)
    rx_delay, window = prepare(s_row, rx_paths, traces, tap_start)
    tx_delay = lax.all_to_all(delay, RX, 0, 0)
    slope, keep, give, path_copy = focus(tx_delay, rx_delay, window, rx_paths)
    got = lax.ppermute(give, "c", swap)
    part = local(pair_sum_kernel, "sum_cores", shaped(*keep.shape), keep, got)
    part = lax.all_to_all(part.reshape(x_size, near, 2 * tx_count, PB), "x", 0, 0)
    rows = (near + 1) * tx_count
    part = local(sum_x_kernel, "sum_x", shaped(2 * near, rows, PB), part)
    part = lax.all_to_all(part, ("zh", "zl"), 0, 0)
    rows = near * (tx_count + 2)
    part, slope_sum = local(
        sum_z_kernel,
        "sum_z",
        [shaped(x_size * lax.axis_size("y"), rows, PB), shaped(tx_count, PB)],
        part,
    )
    part = lax.all_to_all(part, ("x", "y"), 0, 0)
    here = local(sum_y_kernel, "sum_y", shaped(pairs, tx_count + 2, PB), part)
    there = lax.ppermute(here, "c", swap)
    share = gradient(
        tx_count * tx_size,
        tx_size * rx_size,
        patch_cotangent,
        here,
        there,
        pixel_order,
        slope_sum,
        tx_paths,
        slope,
        path_copy,
    )
    share = lax.all_to_all(share, TX + RX, 0, 0, tiled=True)
    return local(total_kernel, "total", shaped(cells), share)


def solution(mesh):
    names = tuple(name for name, _ in FINE)
    fine = Mesh(mesh.devices.reshape([size for _, size in FINE]), names)
    in_specs = (
        P(),
        P(TX, None, RX),
        P(RX, None, None),
        P(TX, RX, None),
        P(TX, RX, None),
        P(),
        P(),
    )
    out_specs = P()
    return jax.shard_map(
        on_device, mesh=fine, in_specs=in_specs, out_specs=out_specs, check_vma=False
    )
```

```python
import math

import jax
import jax.numpy as jnp
from jax import lax
from jax.experimental import pallas as pl
from jax.experimental.pallas import tpu as pltpu
from jax.sharding import Mesh
from jax.sharding import PartitionSpec as P

W = 8
PB = 128
PP = 256
EPS = 1e-06
LN2 = math.log(2.0)
LOG2E = 1.0 / LN2
F32 = jnp.float32
FINE = (("zh", 2), ("y", 4), ("x", 4), ("zl", 4), ("c", 2))
TX = ("zh", "y")
RX = ("x", "zl", "c")


def block_diagonal(s_row, rows, cells):
    wide = jnp.concatenate([s_row] * rows, axis=1)
    shape = (rows, rows * cells)
    owner = lax.broadcasted_iota(jnp.int32, shape, 1) // cells
    mine = owner == lax.broadcasted_iota(jnp.int32, shape, 0)
    return jnp.where(mine, jnp.broadcast_to(wide, shape), 0.0).astype(jnp.bfloat16)


def tx_delay_kernel(s_hbm, path_hbm, out_ref, s_ref, path_ref, copied):
    fetches = [
        pltpu.make_async_copy(s_hbm, s_ref, copied.at[0]),
        pltpu.make_async_copy(path_hbm, path_ref, copied.at[1]),
    ]
    for fetch in fetches:
        fetch.start()
    for fetch in fetches:
        fetch.wait()
    rows, cells, width = path_ref.shape
    left = block_diagonal(s_ref[...].astype(F32), rows, cells)
    delay = jnp.dot(
        left, path_ref[...].reshape(rows * cells, width), preferred_element_type=F32
    )
    out_ref[...] = jnp.broadcast_to((delay * -LOG2E)[None], out_ref.shape)


def prepare_kernel(
    s_hbm,
    path_hbm,
    trace_hbm,
    start_hbm,
    delay_ref,
    win_ref,
    s_ref,
    path_ref,
    trace_ref,
    start_ref,
    sample_ref,
    plain_ref,
    copied,
):
    rx_count, cells, pixels = path_ref.shape
    count = trace_ref.shape[0]
    blocks = start_ref.shape[2]
    per = 128 // blocks
    rows = plain_ref.shape[0]
    groups = rx_count // rows

    fetches = [
        pltpu.make_async_copy(trace_hbm, trace_ref, copied.at[0]),
        pltpu.make_async_copy(start_hbm, start_ref, copied.at[1]),
        pltpu.make_async_copy(s_hbm, s_ref, copied.at[2]),
    ]
    for i in range(groups):
        some = pl.ds(i * rows, rows)
        fetches.append(
            pltpu.make_async_copy(path_hbm.at[some], path_ref.at[some], copied.at[3 + i])
        )
    for fetch in fetches:
        fetch.start()
    for fetch in fetches[:3]:
        fetch.wait()

    sample_ref[...] = trace_ref[...].astype(F32)
    lane_group = lax.broadcasted_iota(jnp.int32, (rows, 128), 1) // blocks

    def windows(step, carry):
        mine = pl.ds(pl.multiple_of(step * rows, rows), rows)
        for early in range(0, count, per):
            picks = []
            for t in range(early, early + per):
                starts = jnp.concatenate([start_ref[t, mine, :]] * per, axis=1)
                for first in range(0, W, per):
                    index = starts + (lane_group + first)
                    low = index & 127
                    high = index >> 7
                    picked = None
                    for part in range(sample_ref.shape[2] // 128):
                        source = sample_ref[t, mine, part * 128 : (part + 1) * 128]
                        got = jnp.take_along_axis(
                            source, low, axis=1, mode="promise_in_bounds"
                        )
                        picked = got if picked is None else jnp.where(high == part, got, picked)
                    picks.append(picked)
            lanes = slice(early * blocks, early * blocks + 128)
            for j in range(W):
                total = None
                for i in range(per):
                    rolled = picks[i * (W // per) + j // per]
                    shift = ((i - j % per) * blocks) % 128
                    if shift:
                        rolled = pltpu.roll(rolled, shift, 1)
                    total = rolled if total is None else jnp.where(lane_group == i, rolled, total)
                win_ref[mine, j, lanes] = total * math.exp(-0.5 * j * j)
        return carry

    lax.fori_loop(0, groups, windows, 0)
    left = block_diagonal(s_ref[...].astype(F32), rows, cells)
    for i in range(groups):
        fetches[3 + i].wait()
        paths = path_ref[i * rows : (i + 1) * rows].reshape(rows * cells, pixels)
        delay = jnp.dot(left, paths, preferred_element_type=F32)
        delay = delay * -LOG2E - (W - 1) / 2.0 * LOG2E
        for k in range(blocks):
            plain_ref[:, k, :] = delay[:, k * PB : (k + 1) * PB]
        for r in range(rows):
            delay_ref[i * rows + r] = jnp.concatenate([plain_ref[r]] * per, axis=0).T


def focus_kernel(
    tx_ref,
    rx_ref,
    win_ref,
    path_ref,
    slope_ref,
    keep_ref,
    give_ref,
    path_copy_ref,
    tx_lane_ref,
    total_f_ref,
    total_s_ref,
    turned_ref,
    copied,
):
    fetch = pltpu.make_async_copy(path_ref, path_copy_ref, copied)
    fetch.start()
    blocks, count, _ = tx_ref.shape
    rows = rx_ref.shape[0]
    per = 128 // blocks
    halves = count // per

    for half in range(halves):
        stack = [tx_ref[:, half * per + i, :] for i in range(per)]
        tx_lane_ref[:, half * 128 : (half + 1) * 128] = jnp.concatenate(stack, axis=0).T
    total_f_ref[...] = jnp.zeros_like(total_f_ref)
    total_s_ref[...] = jnp.zeros_like(total_s_ref)

    def point(tap, tau):
        ratio = jnp.exp2(tau)
        twice = tau + tau
        power = tau * (tau * (-0.5 * LN2) - (W - 1.0))
        focused = None
        for j in range(W - 1, -1, -2):
            upper = jnp.exp2(power)
            lower = upper * ratio
            if focused is None:
                focused = tap[j] * upper
                moment = focused
            else:
                focused = focused + tap[j] * upper
                moment = moment + focused
            focused = focused + tap[j - 1] * lower
            if j > 1:
                moment = moment + focused
                power = power + twice
        return focused, moment * LOG2E + tau * focused

    def receivers(step, carry):
        for half in range(halves):
            lanes = slice(half * 128, (half + 1) * 128)
            taps = [
                [
                    jnp.broadcast_to(win_ref[2 * step + i, j : j + 1, lanes], (8, 128))
                    for j in range(W)
                ]
                for i in range(2)
            ]
            for first in range(0, PB, 8):
                here = slice(first, first + 8)
                total_f = total_f_ref[here, lanes]
                total_s = total_s_ref[here, lanes]
                for i in range(2):
                    tau = tx_lane_ref[here, lanes] + rx_ref[2 * step + i, here, :]
                    focused, slope = point(taps[i], tau)
                    slope_ref[2 * step + i, here, lanes] = slope
                    total_f = total_f + focused
                    total_s = total_s + slope
                total_f_ref[here, lanes] = total_f
                total_s_ref[here, lanes] = total_s
        return carry

    lax.fori_loop(0, rows // 2, receivers, 0)
    mine = lax.axis_index("c")
    for source, base in ((total_f_ref, 0), (total_s_ref, count)):
        for half in range(halves):
            turned_ref[...] = source[:, half * 128 : (half + 1) * 128].T
            for i in range(per):
                row = base + half * per + i
                even = turned_ref[pl.ds(i * blocks, blocks // 2, stride=2), :]
                odd = turned_ref[pl.ds(i * blocks + 1, blocks // 2, stride=2), :]
                keep_ref[:, row, :] = jnp.where(mine == 0, even, odd)
                give_ref[:, row, :] = jnp.where(mine == 0, odd, even)
    fetch.wait()


def pair_sum_kernel(keep_ref, got_ref, out_ref):
    out_ref[...] = keep_ref[...] + got_ref[...]


def sum_x_kernel(part_ref, out_ref):
    sources, blocks, rows, _ = part_ref.shape
    count = rows // 2
    for block in range(blocks):
        total = part_ref[0, block]
        for i in range(1, sources):
            total = total + part_ref[i, block]
        here = slice(block * count, (block + 1) * count)
        beam = total[0:count]
        out_ref[:, here] = jnp.broadcast_to(beam[None], (out_ref.shape[0], count, PB))
        for far in range(out_ref.shape[0] // blocks):
            out_ref[far * blocks + block, blocks * count :] = total[count:rows]


def sum_z_kernel(part_ref, out_ref, slope_sum_ref):
    blocks = 4
    rows = part_ref.shape[1]
    count = rows // (blocks + 1)
    first = lax.axis_index("zh") == 0
    totals = []
    for far in range(part_ref.shape[0] // blocks):
        total = part_ref[far * blocks]
        for i in range(1, blocks):
            total = total + part_ref[far * blocks + i]
        totals.append(total)
    own = jnp.where(first, totals[0], totals[1])
    slope_sum_ref[...] = own[blocks * count :]
    lines = []
    for power in (False, True):
        for block in range(blocks):
            line = None
            for total in totals:
                beam = total[block * count : (block + 1) * count]
                part = jnp.sum(beam * beam if power else beam, axis=0, keepdims=True)
                line = part if line is None else line + part
            lines.append(line)
    wide = out_ref.shape[0]
    out_ref[:, 0 : blocks * count] = jnp.broadcast_to(
        own[0 : blocks * count][None], (wide, blocks * count, PB)
    )
    out_ref[:, blocks * count :] = jnp.broadcast_to(
        jnp.concatenate(lines, axis=0)[None], (wide, 2 * blocks, PB)
    )


def sum_y_kernel(part_ref, out_ref):
    own = lax.axis_index("y")
    sides = 4
    blocks = 4
    count = out_ref.shape[0] - 2
    for x in range(part_ref.shape[0] // sides):
        total = part_ref[x * sides, blocks * count :, :]
        for y in range(1, sides):
            total = total + part_ref[x * sides + y, blocks * count :, :]
        beams = part_ref[x * sides + own, 0 : blocks * count, :]
        for block in range(blocks):
            place = x * blocks + block
            out_ref[0:count, place, :] = beams[block * count : (block + 1) * count]
        here = slice(x * blocks, (x + 1) * blocks)
        out_ref[count, here, :] = total[0:blocks]
        out_ref[count + 1, here, :] = total[blocks : 2 * blocks]


def total_kernel(share_ref, out_ref):
    out_ref[...] = jnp.sum(share_ref[...], axis=0)[0 : out_ref.shape[0]]


def patch_scales(total_tx, cot_ref, ids, coherent, power):
    patches = cot_ref.shape[0]
    square = coherent * coherent
    sums = []
    for field in (square, power):
        rows = [
            jnp.sum(jnp.where(ids == q, field, 0.0), axis=0, keepdims=True)
            for q in range(patches)
        ]
        sums.append(jnp.sum(jnp.concatenate(rows, axis=0), axis=1, keepdims=True))
    numer, power_sum = sums
    denom = total_tx * power_sum
    cot = jnp.zeros_like(numer)
    row = lax.broadcasted_iota(jnp.int32, cot.shape, 0)
    for q in range(patches):
        cot = jnp.where(row == q, cot_ref[q], cot)
    value_n = -2.0 * (cot / (numer + EPS))
    value_d = 2.0 * (cot * total_tx / (denom + EPS))
    scale_n = jnp.zeros_like(square)
    scale_d = jnp.zeros_like(square)
    for q in range(patches):
        inside = ids == q
        scale_n = jnp.where(inside, value_n[q : q + 1, :], scale_n)
        scale_d = jnp.where(inside, value_d[q : q + 1, :], scale_d)
    return scale_n, scale_d


def gradient_kernel(
    total_tx,
    cot_ref,
    here_ref,
    there_ref,
    ids_ref,
    slope_sum_ref,
    tx_path_ref,
    slope_ref,
    path_ref,
    out_ref,
    all_ref,
    bg_ref,
    bg_lane_ref,
    grad_ref,
):
    rows, cells, _ = path_ref.shape
    pairs = here_ref.shape[1]
    blocks = 2 * pairs
    count = slope_sum_ref.shape[0]
    per = 128 // blocks
    together = grad_ref.shape[0]
    core = lax.axis_index("c")
    me = (lax.axis_index("x") * lax.axis_size("zl") + lax.axis_index("zl")) * 2 + core

    for row in range(count + 2):
        here = here_ref[row]
        there = there_ref[row]
        all_ref[row, pl.ds(0, pairs, stride=2), :] = jnp.where(core == 0, here, there)
        all_ref[row, pl.ds(1, pairs, stride=2), :] = jnp.where(core == 0, there, here)
    coherent = all_ref[count]
    power = all_ref[count + 1]
    scale_n, scale_d = patch_scales(total_tx, cot_ref, ids_ref[...] // PP, coherent, power)
    common = coherent * scale_n
    for t in range(count):
        bg_ref[t] = common + all_ref[t] * scale_d
    for half in range(count // per):
        stack = [bg_ref[half * per + i] for i in range(per)]
        bg_lane_ref[:, half * 128 : (half + 1) * 128] = jnp.concatenate(stack, axis=0).T
    start = jnp.zeros((cells, PB), F32)
    for t in range(count):
        own = bg_ref[t, pl.ds(me, 1), :] * slope_sum_ref[t : t + 1, :]
        start = start + tx_path_ref[t].astype(F32) * own

    def receivers(step, acc):
        acc = list(acc)
        for i in range(together):
            r = step * together + i
            grad = None
            for half in range(count // per):
                lanes = slice(half * 128, (half + 1) * 128)
                term = slope_ref[r, :, lanes] * bg_lane_ref[:, lanes]
                grad = term if grad is None else grad + term
            grad = grad.T
            total = grad[0:blocks]
            for group in range(1, per):
                total = total + grad[group * blocks : (group + 1) * blocks]
            grad_ref[i] = total
            for k in range(blocks):
                paths = path_ref[r, :, k * PB : (k + 1) * PB].astype(F32)
                acc[k % 2] = acc[k % 2] + paths * grad_ref[i, k : k + 1, :]
        return tuple(acc)

    acc = lax.fori_loop(0, rows // together, receivers, (start, jnp.zeros_like(start)))
    row = jnp.sum((acc[0] + acc[1]).T, axis=0, keepdims=True) * LN2
    row = jnp.concatenate([row] * (PB // cells), axis=1)
    out_ref[...] = jnp.broadcast_to(row, out_ref.shape)


def params(megabytes):
    return pltpu.CompilerParams(vmem_limit_bytes=megabytes * 1024 * 1024)


def whole(shape):
    return pl.BlockSpec(shape, lambda *_: (0,) * len(shape))


def shaped(*shape):
    return jax.ShapeDtypeStruct(shape, F32)


def in_hbm(array):
    return pltpu.with_memory_space_constraint(array, pltpu.HBM)


def tx_delays(s_row, tx_paths, rx_size):
    tx_count, _, own_pixels = tx_paths.shape
    return pl.pallas_call(
        tx_delay_kernel,
        in_specs=[pl.BlockSpec(memory_space=pl.ANY)] * 2,
        out_shape=shaped(rx_size, tx_count, own_pixels),
        scratch_shapes=[
            pltpu.VMEM(s_row.shape, s_row.dtype),
            pltpu.VMEM(tx_paths.shape, tx_paths.dtype),
            pltpu.SemaphoreType.DMA((2,)),
        ],
        compiler_params=params(4),
        name="tx_delay",
    )(in_hbm(s_row), in_hbm(tx_paths))


def prepare(s_row, rx_paths, traces, tap_start):
    rx_count, cells, pixels = rx_paths.shape
    tx_count, _, samples = traces.shape
    blocks = pixels // PB
    rows = 8
    vmem = pl.BlockSpec(memory_space=pltpu.VMEM)
    arrays = (s_row, rx_paths, traces, tap_start)
    return pl.pallas_call(
        prepare_kernel,
        in_specs=[pl.BlockSpec(memory_space=pl.ANY)] * len(arrays),
        out_specs=[vmem] * 2,
        out_shape=[shaped(rx_count, PB, 128), shaped(rx_count, W, tx_count * blocks)],
        scratch_shapes=[pltpu.VMEM(array.shape, array.dtype) for array in arrays]
        + [
            pltpu.VMEM((tx_count, rx_count, samples), F32),
            pltpu.VMEM((rows, blocks, PB), F32),
            pltpu.SemaphoreType.DMA((len(arrays) - 1 + rx_count // rows,)),
        ],
        compiler_params=params(20),
        name="prepare",
    )(*(in_hbm(array) for array in arrays))


def focus(tx_delay, rx_delay, window, rx_paths):
    blocks, tx_count, _ = tx_delay.shape
    rx_count = rx_delay.shape[0]
    lanes = tx_count * blocks
    vmem = pl.BlockSpec(memory_space=pltpu.VMEM)
    return pl.pallas_call(
        focus_kernel,
        in_specs=[vmem, vmem, vmem, pl.BlockSpec(memory_space=pl.ANY)],
        out_specs=[vmem] * 4,
        out_shape=[
            shaped(rx_count, PB, lanes),
            shaped(blocks // 2, 2 * tx_count, PB),
            shaped(blocks // 2, 2 * tx_count, PB),
            jax.ShapeDtypeStruct(rx_paths.shape, rx_paths.dtype),
        ],
        scratch_shapes=[pltpu.VMEM((PB, lanes), F32)] * 3
        + [pltpu.VMEM((128, PB), F32), pltpu.SemaphoreType.DMA],
        compiler_params=params(20),
        name="focus",
    )(tx_delay, rx_delay, window, in_hbm(rx_paths))


def gradient(total_tx, parts, patch_cotangent, here, there, pixel_order, slope_sum, tx_paths, slope, rx_paths):
    rx_count = rx_paths.shape[0]
    blocks = 2 * here.shape[1]
    tx_count = tx_paths.shape[0]
    lanes = tx_count * blocks
    together = 8
    vmem = pl.BlockSpec(memory_space=pltpu.VMEM)
    return pl.pallas_call(
        lambda *refs: gradient_kernel(total_tx, *refs),
        in_specs=[pl.BlockSpec(memory_space=pltpu.SMEM)] + [vmem] * 7,
        out_specs=vmem,
        out_shape=shaped(parts, PB),
        scratch_shapes=[
            pltpu.VMEM((tx_count + 2, blocks, PB), F32),
            pltpu.VMEM((tx_count, blocks, PB), F32),
            pltpu.VMEM((PB, lanes), F32),
            pltpu.VMEM((together, blocks, PB), F32),
        ],
        compiler_params=params(20),
        name="gradient",
    )(
        patch_cotangent,
        here,
        there,
        pixel_order.reshape(blocks, PB),
        slope_sum,
        tx_paths,
        slope,
        rx_paths,
    )


def local(kernel, name, out_shape, *arrays):
    return pl.pallas_call(
        kernel, out_shape=out_shape, compiler_params=params(4), name=name
    )(*arrays)


def on_device(slowness, tx_paths, rx_paths, traces, tap_start, pixel_order, patch_cotangent):
    tx_count, cells, _ = tx_paths.shape
    rx_size = lax.axis_size(RX)
    tx_size = lax.axis_size(TX)
    x_size = lax.axis_size("x")
    near = lax.axis_size("zl")
    pairs = x_size * near
    s_row = slowness.reshape(1, cells)
    swap = [(0, 1), (1, 0)]

    delay = tx_delays(s_row, tx_paths, rx_size)
    rx_delay, window = prepare(s_row, rx_paths, traces, tap_start)
    tx_delay = lax.all_to_all(delay, RX, 0, 0)
    slope, keep, give, path_copy = focus(tx_delay, rx_delay, window, rx_paths)
    got = lax.ppermute(give, "c", swap)
    part = local(pair_sum_kernel, "sum_cores", shaped(*keep.shape), keep, got)
    part = lax.all_to_all(part.reshape(x_size, near, 2 * tx_count, PB), "x", 0, 0)
    rows = (near + 1) * tx_count
    part = local(sum_x_kernel, "sum_x", shaped(2 * near, rows, PB), part)
    part = lax.all_to_all(part, ("zh", "zl"), 0, 0)
    rows = near * (tx_count + 2)
    part, slope_sum = local(
        sum_z_kernel,
        "sum_z",
        [shaped(x_size * lax.axis_size("y"), rows, PB), shaped(tx_count, PB)],
        part,
    )
    part = lax.all_to_all(part, ("x", "y"), 0, 0)
    here = local(sum_y_kernel, "sum_y", shaped(tx_count + 2, pairs, PB), part)
    there = lax.ppermute(here, "c", swap)
    share = gradient(
        tx_count * tx_size,
        tx_size * rx_size,
        patch_cotangent,
        here,
        there,
        pixel_order,
        slope_sum,
        tx_paths,
        slope,
        path_copy,
    )
    share = lax.all_to_all(share, TX + RX, 0, 0, tiled=True)
    return local(total_kernel, "total", shaped(cells), share)


def solution(mesh):
    names = tuple(name for name, _ in FINE)
    fine = Mesh(mesh.devices.reshape([size for _, size in FINE]), names)
    in_specs = (
        P(),
        P(TX, None, RX),
        P(RX, None, None),
        P(TX, RX, None),
        P(TX, RX, None),
        P(),
        P(),
    )
    out_specs = P()
    return jax.shard_map(
        on_device, mesh=fine, in_specs=in_specs, out_specs=out_specs, check_vma=False
    )
```

```python
import math

import jax
import jax.numpy as jnp
import numpy as np
from jax import lax
from jax.experimental import pallas as pl
from jax.experimental.pallas import tpu as pltpu
from jax.sharding import Mesh
from jax.sharding import PartitionSpec as P

W = 8
PB = 128
PP = 256
EPS = 1e-06
LN2 = math.log(2.0)
LOG2E = 1.0 / LN2
F32 = jnp.float32
FINE = (("zh", 2), ("y", 4), ("x", 4), ("zl", 4), ("c", 2))
EVERY = tuple(name for name, _ in FINE)
X_ORDER = (0, 2, 1, 3)
Z_ORDER = (0, 4, 2, 6, 1, 5, 3, 7)
TX = ("zh", "y")
RX = ("x", "zl", "c")


def block_diagonal(s_row, rows, cells):
    wide = jnp.concatenate([s_row] * rows, axis=1)
    shape = (rows, rows * cells)
    owner = lax.broadcasted_iota(jnp.int32, shape, 1) // cells
    mine = owner == lax.broadcasted_iota(jnp.int32, shape, 0)
    return jnp.where(mine, jnp.broadcast_to(wide, shape), 0.0).astype(jnp.bfloat16)


def tx_delay_kernel(s_hbm, path_hbm, out_ref, s_ref, path_ref, copied):
    fetches = [
        pltpu.make_async_copy(s_hbm, s_ref, copied.at[0]),
        pltpu.make_async_copy(path_hbm, path_ref, copied.at[1]),
    ]
    for fetch in fetches:
        fetch.start()
    for fetch in fetches:
        fetch.wait()
    rows, cells, width = path_ref.shape
    left = block_diagonal(s_ref[...].astype(F32), rows, cells)
    delay = jnp.dot(
        left, path_ref[...].reshape(rows * cells, width), preferred_element_type=F32
    )
    out_ref[...] = jnp.broadcast_to((delay * -LOG2E)[None], out_ref.shape)


def prepare_kernel(
    s_hbm,
    path_hbm,
    trace_hbm,
    start_hbm,
    delay_ref,
    win_ref,
    s_ref,
    path_ref,
    trace_ref,
    start_ref,
    sample_ref,
    plain_ref,
    copied,
):
    rx_count, cells, pixels = path_ref.shape
    count = trace_ref.shape[0]
    blocks = start_ref.shape[2]
    per = 128 // blocks
    rows = plain_ref.shape[0]
    groups = rx_count // rows

    fetches = [
        pltpu.make_async_copy(trace_hbm, trace_ref, copied.at[0]),
        pltpu.make_async_copy(start_hbm, start_ref, copied.at[1]),
        pltpu.make_async_copy(s_hbm, s_ref, copied.at[2]),
    ]
    for i in range(groups):
        some = pl.ds(i * rows, rows)
        fetches.append(
            pltpu.make_async_copy(path_hbm.at[some], path_ref.at[some], copied.at[3 + i])
        )
    for fetch in fetches:
        fetch.start()
    for fetch in fetches[:3]:
        fetch.wait()

    sample_ref[...] = trace_ref[...].astype(F32)
    lane_group = lax.broadcasted_iota(jnp.int32, (rows, 128), 1) // blocks

    def windows(step, carry):
        mine = pl.ds(pl.multiple_of(step * rows, rows), rows)
        for early in range(0, count, per):
            picks = []
            for t in range(early, early + per):
                starts = jnp.concatenate([start_ref[t, mine, :]] * per, axis=1)
                for first in range(0, W, per):
                    index = starts + (lane_group + first)
                    low = index & 127
                    high = index >> 7
                    picked = None
                    for part in range(sample_ref.shape[2] // 128):
                        source = sample_ref[t, mine, part * 128 : (part + 1) * 128]
                        got = jnp.take_along_axis(
                            source, low, axis=1, mode="promise_in_bounds"
                        )
                        picked = got if picked is None else jnp.where(high == part, got, picked)
                    picks.append(picked)
            lanes = slice(early * blocks, early * blocks + 128)
            for j in range(W):
                total = None
                for i in range(per):
                    rolled = picks[i * (W // per) + j // per]
                    shift = ((i - j % per) * blocks) % 128
                    if shift:
                        rolled = pltpu.roll(rolled, shift, 1)
                    total = rolled if total is None else jnp.where(lane_group == i, rolled, total)
                win_ref[mine, j, lanes] = total * math.exp(-0.5 * j * j)
        return carry

    lax.fori_loop(0, groups, windows, 0)
    left = block_diagonal(s_ref[...].astype(F32), rows, cells)
    for i in range(groups):
        fetches[3 + i].wait()
        paths = path_ref[i * rows : (i + 1) * rows].reshape(rows * cells, pixels)
        delay = jnp.dot(left, paths, preferred_element_type=F32)
        delay = delay * -LOG2E - (W - 1) / 2.0 * LOG2E
        for k in range(blocks):
            plain_ref[:, k, :] = delay[:, k * PB : (k + 1) * PB]
        for r in range(rows):
            delay_ref[i * rows + r] = jnp.concatenate([plain_ref[r]] * per, axis=0).T


def focus_kernel(
    tx_ref,
    rx_ref,
    win_ref,
    path_ref,
    slope_ref,
    keep_ref,
    give_ref,
    path_copy_ref,
    tx_lane_ref,
    total_f_ref,
    total_s_ref,
    turned_ref,
    copied,
):
    fetch = pltpu.make_async_copy(path_ref, path_copy_ref, copied)
    fetch.start()
    blocks, count, _ = tx_ref.shape
    rows = rx_ref.shape[0]
    per = 128 // blocks
    halves = count // per

    for half in range(halves):
        stack = [tx_ref[:, half * per + i, :] for i in range(per)]
        tx_lane_ref[:, half * 128 : (half + 1) * 128] = jnp.concatenate(stack, axis=0).T
    total_f_ref[...] = jnp.zeros_like(total_f_ref)
    total_s_ref[...] = jnp.zeros_like(total_s_ref)

    def point(tap, tau):
        ratio = jnp.exp2(tau)
        twice = tau + tau
        power = tau * (tau * (-0.5 * LN2) - (W - 1.0))
        focused = None
        for j in range(W - 1, -1, -2):
            upper = jnp.exp2(power)
            lower = upper * ratio
            if focused is None:
                focused = tap[j] * upper
                moment = focused
            else:
                focused = focused + tap[j] * upper
                moment = moment + focused
            focused = focused + tap[j - 1] * lower
            if j > 1:
                moment = moment + focused
                power = power + twice
        return focused, moment * LOG2E + tau * focused

    def receivers(step, carry):
        for half in range(halves):
            lanes = slice(half * 128, (half + 1) * 128)
            taps = [
                [
                    jnp.broadcast_to(win_ref[2 * step + i, j : j + 1, lanes], (8, 128))
                    for j in range(W)
                ]
                for i in range(2)
            ]
            for first in range(0, PB, 8):
                here = slice(first, first + 8)
                total_f = total_f_ref[here, lanes]
                total_s = total_s_ref[here, lanes]
                for i in range(2):
                    tau = tx_lane_ref[here, lanes] + rx_ref[2 * step + i, here, :]
                    focused, slope = point(taps[i], tau)
                    slope_ref[2 * step + i, here, lanes] = slope
                    total_f = total_f + focused
                    total_s = total_s + slope
                total_f_ref[here, lanes] = total_f
                total_s_ref[here, lanes] = total_s
        return carry

    lax.fori_loop(0, rows // 2, receivers, 0)
    mine = lax.axis_index("c")
    for source, base in ((total_f_ref, 0), (total_s_ref, count)):
        for half in range(halves):
            turned_ref[...] = source[:, half * 128 : (half + 1) * 128].T
            for i in range(per):
                row = base + half * per + i
                even = turned_ref[pl.ds(i * blocks, blocks // 2, stride=2), :]
                odd = turned_ref[pl.ds(i * blocks + 1, blocks // 2, stride=2), :]
                keep_ref[:, row, :] = jnp.where(mine == 0, even, odd)
                give_ref[:, row, :] = jnp.where(mine == 0, odd, even)
    fetch.wait()


def pair_sum_kernel(keep_ref, got_ref, out_ref):
    near = out_ref.shape[0] // len(X_ORDER)
    for place, x in enumerate(X_ORDER):
        some = slice(x * near, (x + 1) * near)
        out_ref[place * near : (place + 1) * near] = keep_ref[some] + got_ref[some]


def sum_x_kernel(part_ref, out_ref):
    sources, blocks, rows, _ = part_ref.shape
    count = rows // 2
    for block in range(blocks):
        total = part_ref[0, block]
        for i in range(1, sources):
            total = total + part_ref[i, block]
        here = slice(block * count, (block + 1) * count)
        beam = total[0:count]
        out_ref[:, here] = jnp.broadcast_to(beam[None], (out_ref.shape[0], count, PB))
        for place, z in enumerate(Z_ORDER):
            if z % blocks == block:
                out_ref[place, blocks * count :] = total[count:rows]


def sum_z_kernel(part_ref, out_ref, slope_sum_ref):
    blocks = 4
    rows = part_ref.shape[1]
    count = rows // (blocks + 1)
    first = lax.axis_index("zh") == 0
    totals = []
    for far in range(part_ref.shape[0] // blocks):
        total = None
        for place, z in enumerate(Z_ORDER):
            if z // blocks == far:
                total = part_ref[place] if total is None else total + part_ref[place]
        totals.append(total)
    own = jnp.where(first, totals[0], totals[1])
    slope_sum_ref[...] = own[blocks * count :]
    lines = []
    for power in (False, True):
        for block in range(blocks):
            line = None
            for total in totals:
                beam = total[block * count : (block + 1) * count]
                part = jnp.sum(beam * beam if power else beam, axis=0, keepdims=True)
                line = part if line is None else line + part
            lines.append(line)
    wide = out_ref.shape[0]
    out_ref[:, 0 : blocks * count] = jnp.broadcast_to(
        own[0 : blocks * count][None], (wide, blocks * count, PB)
    )
    out_ref[:, blocks * count :] = jnp.broadcast_to(
        jnp.concatenate(lines, axis=0)[None], (wide, 2 * blocks, PB)
    )


def sum_y_kernel(part_ref, out_ref):
    own = lax.axis_index("y")
    sides = 4
    blocks = 4
    count = out_ref.shape[0] - 2
    for x in range(part_ref.shape[0] // sides):
        total = part_ref[x * sides, blocks * count :, :]
        for y in range(1, sides):
            total = total + part_ref[x * sides + y, blocks * count :, :]
        beams = part_ref[x * sides + own, 0 : blocks * count, :]
        for block in range(blocks):
            place = x * blocks + block
            out_ref[0:count, place, :] = beams[block * count : (block + 1) * count]
        here = slice(x * blocks, (x + 1) * blocks)
        out_ref[count, here, :] = total[0:blocks]
        out_ref[count + 1, here, :] = total[blocks : 2 * blocks]


def total_kernel(share_ref, out_ref):
    out_ref[...] = jnp.sum(share_ref[...], axis=0)[0 : out_ref.shape[0]]


def patch_scales(total_tx, cot_ref, ids, coherent, power):
    patches = cot_ref.shape[0]
    square = coherent * coherent
    sums = []
    for field in (square, power):
        rows = [
            jnp.sum(jnp.where(ids == q, field, 0.0), axis=0, keepdims=True)
            for q in range(patches)
        ]
        sums.append(jnp.sum(jnp.concatenate(rows, axis=0), axis=1, keepdims=True))
    numer, power_sum = sums
    denom = total_tx * power_sum
    cot = jnp.zeros_like(numer)
    row = lax.broadcasted_iota(jnp.int32, cot.shape, 0)
    for q in range(patches):
        cot = jnp.where(row == q, cot_ref[q], cot)
    value_n = -2.0 * (cot / (numer + EPS))
    value_d = 2.0 * (cot * total_tx / (denom + EPS))
    scale_n = jnp.zeros_like(square)
    scale_d = jnp.zeros_like(square)
    for q in range(patches):
        inside = ids == q
        scale_n = jnp.where(inside, value_n[q : q + 1, :], scale_n)
        scale_d = jnp.where(inside, value_d[q : q + 1, :], scale_d)
    return scale_n, scale_d


def gradient_kernel(
    total_tx,
    cot_ref,
    here_ref,
    there_ref,
    ids_ref,
    slope_sum_ref,
    tx_path_ref,
    slope_ref,
    path_ref,
    out_ref,
    all_ref,
    bg_ref,
    bg_lane_ref,
    grad_ref,
):
    rows, cells, _ = path_ref.shape
    pairs = here_ref.shape[1]
    blocks = 2 * pairs
    count = slope_sum_ref.shape[0]
    per = 128 // blocks
    together = grad_ref.shape[0]
    core = lax.axis_index("c")
    me = (lax.axis_index("x") * lax.axis_size("zl") + lax.axis_index("zl")) * 2 + core

    for row in range(count + 2):
        here = here_ref[row]
        there = there_ref[row]
        all_ref[row, pl.ds(0, pairs, stride=2), :] = jnp.where(core == 0, here, there)
        all_ref[row, pl.ds(1, pairs, stride=2), :] = jnp.where(core == 0, there, here)
    coherent = all_ref[count]
    power = all_ref[count + 1]
    scale_n, scale_d = patch_scales(total_tx, cot_ref, ids_ref[...] // PP, coherent, power)
    common = coherent * scale_n
    for t in range(count):
        bg_ref[t] = common + all_ref[t] * scale_d
    for half in range(count // per):
        stack = [bg_ref[half * per + i] for i in range(per)]
        bg_lane_ref[:, half * 128 : (half + 1) * 128] = jnp.concatenate(stack, axis=0).T
    start = jnp.zeros((cells, PB), F32)
    for t in range(count):
        own = bg_ref[t, pl.ds(me, 1), :] * slope_sum_ref[t : t + 1, :]
        start = start + tx_path_ref[t].astype(F32) * own

    def receivers(step, acc):
        acc = list(acc)
        for i in range(together):
            r = step * together + i
            grad = None
            for half in range(count // per):
                lanes = slice(half * 128, (half + 1) * 128)
                term = slope_ref[r, :, lanes] * bg_lane_ref[:, lanes]
                grad = term if grad is None else grad + term
            grad = grad.T
            total = grad[0:blocks]
            for group in range(1, per):
                total = total + grad[group * blocks : (group + 1) * blocks]
            grad_ref[i] = total
            for k in range(blocks):
                paths = path_ref[r, :, k * PB : (k + 1) * PB].astype(F32)
                acc[k % 2] = acc[k % 2] + paths * grad_ref[i, k : k + 1, :]
        return tuple(acc)

    acc = lax.fori_loop(0, rows // together, receivers, (start, jnp.zeros_like(start)))
    row = jnp.sum((acc[0] + acc[1]).T, axis=0, keepdims=True) * LN2
    row = jnp.concatenate([row] * (PB // cells), axis=1)
    out_ref[...] = jnp.broadcast_to(row, out_ref.shape)


def groups_along(axes, order):
    sizes = [size for _, size in FINE]
    ids = np.arange(math.prod(sizes)).reshape(sizes)
    moved = [EVERY.index(axis) for axis in axes]
    ids = np.moveaxis(ids, moved, range(-len(moved), 0)).reshape(-1, len(order))
    return ids[:, list(order)].tolist()


def exchange(array, axes, order):
    return lax.all_to_all(array, EVERY, 0, 0, axis_index_groups=groups_along(axes, order))


def params(megabytes):
    return pltpu.CompilerParams(vmem_limit_bytes=megabytes * 1024 * 1024)


def whole(shape):
    return pl.BlockSpec(shape, lambda *_: (0,) * len(shape))


def shaped(*shape):
    return jax.ShapeDtypeStruct(shape, F32)


def in_hbm(array):
    return pltpu.with_memory_space_constraint(array, pltpu.HBM)


def tx_delays(s_row, tx_paths, rx_size):
    tx_count, _, own_pixels = tx_paths.shape
    return pl.pallas_call(
        tx_delay_kernel,
        in_specs=[pl.BlockSpec(memory_space=pl.ANY)] * 2,
        out_shape=shaped(rx_size, tx_count, own_pixels),
        scratch_shapes=[
            pltpu.VMEM(s_row.shape, s_row.dtype),
            pltpu.VMEM(tx_paths.shape, tx_paths.dtype),
            pltpu.SemaphoreType.DMA((2,)),
        ],
        compiler_params=params(4),
        name="tx_delay",
    )(in_hbm(s_row), in_hbm(tx_paths))


def prepare(s_row, rx_paths, traces, tap_start):
    rx_count, cells, pixels = rx_paths.shape
    tx_count, _, samples = traces.shape
    blocks = pixels // PB
    rows = 8
    vmem = pl.BlockSpec(memory_space=pltpu.VMEM)
    arrays = (s_row, rx_paths, traces, tap_start)
    return pl.pallas_call(
        prepare_kernel,
        in_specs=[pl.BlockSpec(memory_space=pl.ANY)] * len(arrays),
        out_specs=[vmem] * 2,
        out_shape=[shaped(rx_count, PB, 128), shaped(rx_count, W, tx_count * blocks)],
        scratch_shapes=[pltpu.VMEM(array.shape, array.dtype) for array in arrays]
        + [
            pltpu.VMEM((tx_count, rx_count, samples), F32),
            pltpu.VMEM((rows, blocks, PB), F32),
            pltpu.SemaphoreType.DMA((len(arrays) - 1 + rx_count // rows,)),
        ],
        compiler_params=params(20),
        name="prepare",
    )(*(in_hbm(array) for array in arrays))


def focus(tx_delay, rx_delay, window, rx_paths):
    blocks, tx_count, _ = tx_delay.shape
    rx_count = rx_delay.shape[0]
    lanes = tx_count * blocks
    vmem = pl.BlockSpec(memory_space=pltpu.VMEM)
    return pl.pallas_call(
        focus_kernel,
        in_specs=[vmem, vmem, vmem, pl.BlockSpec(memory_space=pl.ANY)],
        out_specs=[vmem] * 4,
        out_shape=[
            shaped(rx_count, PB, lanes),
            shaped(blocks // 2, 2 * tx_count, PB),
            shaped(blocks // 2, 2 * tx_count, PB),
            jax.ShapeDtypeStruct(rx_paths.shape, rx_paths.dtype),
        ],
        scratch_shapes=[pltpu.VMEM((PB, lanes), F32)] * 3
        + [pltpu.VMEM((128, PB), F32), pltpu.SemaphoreType.DMA],
        compiler_params=params(20),
        name="focus",
    )(tx_delay, rx_delay, window, in_hbm(rx_paths))


def gradient(total_tx, parts, patch_cotangent, here, there, pixel_order, slope_sum, tx_paths, slope, rx_paths):
    rx_count = rx_paths.shape[0]
    blocks = 2 * here.shape[1]
    tx_count = tx_paths.shape[0]
    lanes = tx_count * blocks
    together = 8
    vmem = pl.BlockSpec(memory_space=pltpu.VMEM)
    return pl.pallas_call(
        lambda *refs: gradient_kernel(total_tx, *refs),
        in_specs=[pl.BlockSpec(memory_space=pltpu.SMEM)] + [vmem] * 7,
        out_specs=vmem,
        out_shape=shaped(parts, PB),
        scratch_shapes=[
            pltpu.VMEM((tx_count + 2, blocks, PB), F32),
            pltpu.VMEM((tx_count, blocks, PB), F32),
            pltpu.VMEM((PB, lanes), F32),
            pltpu.VMEM((together, blocks, PB), F32),
        ],
        compiler_params=params(20),
        name="gradient",
    )(
        patch_cotangent,
        here,
        there,
        pixel_order.reshape(blocks, PB),
        slope_sum,
        tx_paths,
        slope,
        rx_paths,
    )


def local(kernel, name, out_shape, *arrays):
    return pl.pallas_call(
        kernel, out_shape=out_shape, compiler_params=params(4), name=name
    )(*arrays)


def on_device(slowness, tx_paths, rx_paths, traces, tap_start, pixel_order, patch_cotangent):
    tx_count, cells, _ = tx_paths.shape
    rx_size = lax.axis_size(RX)
    tx_size = lax.axis_size(TX)
    x_size = lax.axis_size("x")
    near = lax.axis_size("zl")
    pairs = x_size * near
    s_row = slowness.reshape(1, cells)
    swap = [(0, 1), (1, 0)]

    delay = tx_delays(s_row, tx_paths, rx_size)
    rx_delay, window = prepare(s_row, rx_paths, traces, tap_start)
    tx_delay = lax.all_to_all(delay, RX, 0, 0)
    slope, keep, give, path_copy = focus(tx_delay, rx_delay, window, rx_paths)
    got = lax.ppermute(give, "c", swap)
    part = local(pair_sum_kernel, "sum_cores", shaped(*keep.shape), keep, got)
    part = exchange(part.reshape(x_size, near, 2 * tx_count, PB), ("x",), X_ORDER)
    rows = (near + 1) * tx_count
    part = local(sum_x_kernel, "sum_x", shaped(2 * near, rows, PB), part)
    part = exchange(part, ("zh", "zl"), Z_ORDER)
    rows = near * (tx_count + 2)
    part, slope_sum = local(
        sum_z_kernel,
        "sum_z",
        [shaped(x_size * lax.axis_size("y"), rows, PB), shaped(tx_count, PB)],
        part,
    )
    part = lax.all_to_all(part, ("x", "y"), 0, 0)
    here = local(sum_y_kernel, "sum_y", shaped(tx_count + 2, pairs, PB), part)
    there = lax.ppermute(here, "c", swap)
    share = gradient(
        tx_count * tx_size,
        tx_size * rx_size,
        patch_cotangent,
        here,
        there,
        pixel_order,
        slope_sum,
        tx_paths,
        slope,
        path_copy,
    )
    share = lax.all_to_all(share, TX + RX, 0, 0, tiled=True)
    return local(total_kernel, "total", shaped(cells), share)


def solution(mesh):
    fine = Mesh(mesh.devices.reshape([size for _, size in FINE]), EVERY)
    in_specs = (
        P(),
        P(TX, None, RX),
        P(RX, None, None),
        P(TX, RX, None),
        P(TX, RX, None),
        P(),
        P(),
    )
    out_specs = P()
    return jax.shard_map(
        on_device, mesh=fine, in_specs=in_specs, out_specs=out_specs, check_vma=False
    )
```

```python
import math

import jax
import jax.numpy as jnp
import numpy as np
from jax import lax
from jax.experimental import pallas as pl
from jax.experimental.pallas import tpu as pltpu
from jax.sharding import Mesh
from jax.sharding import PartitionSpec as P

W = 8
PB = 128
PP = 256
EPS = 1e-06
LN2 = math.log(2.0)
LOG2E = 1.0 / LN2
F32 = jnp.float32
FINE = (("zh", 2), ("y", 4), ("x", 4), ("zl", 4), ("c", 2))
EVERY = tuple(name for name, _ in FINE)
X_ORDER = (0, 2, 1, 3)
Z_ORDER = (0, 2, 5, 7, 4, 6, 1, 3)
TX = ("zh", "y")
RX = ("x", "zl", "c")


def block_diagonal(s_row, rows, cells):
    wide = jnp.concatenate([s_row] * rows, axis=1)
    shape = (rows, rows * cells)
    owner = lax.broadcasted_iota(jnp.int32, shape, 1) // cells
    mine = owner == lax.broadcasted_iota(jnp.int32, shape, 0)
    return jnp.where(mine, jnp.broadcast_to(wide, shape), 0.0).astype(jnp.bfloat16)


def tx_delay_kernel(s_hbm, path_hbm, out_ref, s_ref, path_ref, copied):
    fetches = [
        pltpu.make_async_copy(s_hbm, s_ref, copied.at[0]),
        pltpu.make_async_copy(path_hbm, path_ref, copied.at[1]),
    ]
    for fetch in fetches:
        fetch.start()
    for fetch in fetches:
        fetch.wait()
    rows, cells, width = path_ref.shape
    left = block_diagonal(s_ref[...].astype(F32), rows, cells)
    delay = jnp.dot(
        left, path_ref[...].reshape(rows * cells, width), preferred_element_type=F32
    )
    out_ref[...] = jnp.broadcast_to((delay * -LOG2E)[None], out_ref.shape)


def prepare_kernel(
    s_hbm,
    path_hbm,
    trace_hbm,
    start_hbm,
    delay_ref,
    win_ref,
    s_ref,
    path_ref,
    trace_ref,
    start_ref,
    sample_ref,
    plain_ref,
    copied,
):
    rx_count, cells, pixels = path_ref.shape
    count = trace_ref.shape[0]
    blocks = start_ref.shape[2]
    per = 128 // blocks
    rows = plain_ref.shape[0]
    groups = rx_count // rows

    fetches = [
        pltpu.make_async_copy(trace_hbm, trace_ref, copied.at[0]),
        pltpu.make_async_copy(start_hbm, start_ref, copied.at[1]),
        pltpu.make_async_copy(s_hbm, s_ref, copied.at[2]),
    ]
    for i in range(groups):
        some = pl.ds(i * rows, rows)
        fetches.append(
            pltpu.make_async_copy(path_hbm.at[some], path_ref.at[some], copied.at[3 + i])
        )
    for fetch in fetches:
        fetch.start()
    for fetch in fetches[:3]:
        fetch.wait()

    sample_ref[...] = trace_ref[...].astype(F32)
    lane_group = lax.broadcasted_iota(jnp.int32, (rows, 128), 1) // blocks

    def windows(step, carry):
        mine = pl.ds(pl.multiple_of(step * rows, rows), rows)
        for early in range(0, count, per):
            picks = []
            for t in range(early, early + per):
                starts = jnp.concatenate([start_ref[t, mine, :]] * per, axis=1)
                for first in range(0, W, per):
                    index = starts + (lane_group + first)
                    low = index & 127
                    high = index >> 7
                    picked = None
                    for part in range(sample_ref.shape[2] // 128):
                        source = sample_ref[t, mine, part * 128 : (part + 1) * 128]
                        got = jnp.take_along_axis(
                            source, low, axis=1, mode="promise_in_bounds"
                        )
                        picked = got if picked is None else jnp.where(high == part, got, picked)
                    picks.append(picked)
            lanes = slice(early * blocks, early * blocks + 128)
            for j in range(W):
                total = None
                for i in range(per):
                    rolled = picks[i * (W // per) + j // per]
                    shift = ((i - j % per) * blocks) % 128
                    if shift:
                        rolled = pltpu.roll(rolled, shift, 1)
                    total = rolled if total is None else jnp.where(lane_group == i, rolled, total)
                win_ref[mine, j, lanes] = total * math.exp(-0.5 * j * j)
        return carry

    lax.fori_loop(0, groups, windows, 0)
    left = block_diagonal(s_ref[...].astype(F32), rows, cells)
    for i in range(groups):
        fetches[3 + i].wait()
        paths = path_ref[i * rows : (i + 1) * rows].reshape(rows * cells, pixels)
        delay = jnp.dot(left, paths, preferred_element_type=F32)
        delay = delay * -LOG2E - (W - 1) / 2.0 * LOG2E
        for k in range(blocks):
            plain_ref[:, k, :] = delay[:, k * PB : (k + 1) * PB]
        for r in range(rows):
            delay_ref[i * rows + r] = jnp.concatenate([plain_ref[r]] * per, axis=0).T


def focus_kernel(
    tx_ref,
    rx_ref,
    win_ref,
    path_ref,
    slope_ref,
    keep_ref,
    give_ref,
    path_copy_ref,
    tx_lane_ref,
    total_f_ref,
    total_s_ref,
    turned_ref,
    copied,
):
    fetch = pltpu.make_async_copy(path_ref, path_copy_ref, copied)
    fetch.start()
    blocks, count, _ = tx_ref.shape
    rows = rx_ref.shape[0]
    per = 128 // blocks
    halves = count // per

    for half in range(halves):
        stack = [tx_ref[:, half * per + i, :] for i in range(per)]
        tx_lane_ref[:, half * 128 : (half + 1) * 128] = jnp.concatenate(stack, axis=0).T
    total_f_ref[...] = jnp.zeros_like(total_f_ref)
    total_s_ref[...] = jnp.zeros_like(total_s_ref)

    def point(tap, tau):
        ratio = jnp.exp2(tau)
        twice = tau + tau
        power = tau * (tau * (-0.5 * LN2) - (W - 1.0))
        focused = None
        for j in range(W - 1, -1, -2):
            upper = jnp.exp2(power)
            lower = upper * ratio
            if focused is None:
                focused = tap[j] * upper
                moment = focused
            else:
                focused = focused + tap[j] * upper
                moment = moment + focused
            focused = focused + tap[j - 1] * lower
            if j > 1:
                moment = moment + focused
                power = power + twice
        return focused, moment * LOG2E + tau * focused

    def receivers(step, carry):
        for half in range(halves):
            lanes = slice(half * 128, (half + 1) * 128)
            taps = [
                [
                    jnp.broadcast_to(win_ref[2 * step + i, j : j + 1, lanes], (8, 128))
                    for j in range(W)
                ]
                for i in range(2)
            ]
            for first in range(0, PB, 8):
                here = slice(first, first + 8)
                total_f = total_f_ref[here, lanes]
                total_s = total_s_ref[here, lanes]
                for i in range(2):
                    tau = tx_lane_ref[here, lanes] + rx_ref[2 * step + i, here, :]
                    focused, slope = point(taps[i], tau)
                    slope_ref[2 * step + i, here, lanes] = slope
                    total_f = total_f + focused
                    total_s = total_s + slope
                total_f_ref[here, lanes] = total_f
                total_s_ref[here, lanes] = total_s
        return carry

    lax.fori_loop(0, rows // 2, receivers, 0)
    mine = lax.axis_index("c")
    for source, base in ((total_f_ref, 0), (total_s_ref, count)):
        for half in range(halves):
            turned_ref[...] = source[:, half * 128 : (half + 1) * 128].T
            for i in range(per):
                row = base + half * per + i
                even = turned_ref[pl.ds(i * blocks, blocks // 2, stride=2), :]
                odd = turned_ref[pl.ds(i * blocks + 1, blocks // 2, stride=2), :]
                keep_ref[:, row, :] = jnp.where(mine == 0, even, odd)
                give_ref[:, row, :] = jnp.where(mine == 0, odd, even)
    fetch.wait()


def pair_sum_kernel(keep_ref, got_ref, out_ref):
    near = out_ref.shape[0] // len(X_ORDER)
    for place, x in enumerate(X_ORDER):
        some = slice(x * near, (x + 1) * near)
        out_ref[place * near : (place + 1) * near] = keep_ref[some] + got_ref[some]


def sum_x_kernel(part_ref, out_ref):
    sources, blocks, rows, _ = part_ref.shape
    count = rows // 2
    for block in range(blocks):
        total = part_ref[0, block]
        for i in range(1, sources):
            total = total + part_ref[i, block]
        here = slice(block * count, (block + 1) * count)
        beam = total[0:count]
        out_ref[:, here] = jnp.broadcast_to(beam[None], (out_ref.shape[0], count, PB))
        for place, z in enumerate(Z_ORDER):
            if z % blocks == block:
                out_ref[place, blocks * count :] = total[count:rows]


def sum_z_kernel(part_ref, out_ref, slope_sum_ref):
    blocks = 4
    rows = part_ref.shape[1]
    count = rows // (blocks + 1)
    first = lax.axis_index("zh") == 0
    totals = []
    for far in range(part_ref.shape[0] // blocks):
        total = None
        for place, z in enumerate(Z_ORDER):
            if z // blocks == far:
                total = part_ref[place] if total is None else total + part_ref[place]
        totals.append(total)
    own = jnp.where(first, totals[0], totals[1])
    slope_sum_ref[...] = own[blocks * count :]
    lines = []
    for power in (False, True):
        for block in range(blocks):
            line = None
            for total in totals:
                beam = total[block * count : (block + 1) * count]
                part = jnp.sum(beam * beam if power else beam, axis=0, keepdims=True)
                line = part if line is None else line + part
            lines.append(line)
    wide = out_ref.shape[0]
    out_ref[:, 0 : blocks * count] = jnp.broadcast_to(
        own[0 : blocks * count][None], (wide, blocks * count, PB)
    )
    out_ref[:, blocks * count :] = jnp.broadcast_to(
        jnp.concatenate(lines, axis=0)[None], (wide, 2 * blocks, PB)
    )


def sum_y_kernel(part_ref, out_ref):
    own = lax.axis_index("y")
    sides = 4
    blocks = 4
    count = out_ref.shape[0] - 2
    for x in range(part_ref.shape[0] // sides):
        total = part_ref[x * sides, blocks * count :, :]
        for y in range(1, sides):
            total = total + part_ref[x * sides + y, blocks * count :, :]
        beams = part_ref[x * sides + own, 0 : blocks * count, :]
        for block in range(blocks):
            place = x * blocks + block
            out_ref[0:count, place, :] = beams[block * count : (block + 1) * count]
        here = slice(x * blocks, (x + 1) * blocks)
        out_ref[count, here, :] = total[0:blocks]
        out_ref[count + 1, here, :] = total[blocks : 2 * blocks]


def total_kernel(share_ref, out_ref):
    out_ref[...] = jnp.sum(share_ref[...], axis=0)[0 : out_ref.shape[0]]


def patch_scales(total_tx, cot_ref, ids, coherent, power):
    patches = cot_ref.shape[0]
    square = coherent * coherent
    sums = []
    for field in (square, power):
        rows = [
            jnp.sum(jnp.where(ids == q, field, 0.0), axis=0, keepdims=True)
            for q in range(patches)
        ]
        sums.append(jnp.sum(jnp.concatenate(rows, axis=0), axis=1, keepdims=True))
    numer, power_sum = sums
    denom = total_tx * power_sum
    cot = jnp.zeros_like(numer)
    row = lax.broadcasted_iota(jnp.int32, cot.shape, 0)
    for q in range(patches):
        cot = jnp.where(row == q, cot_ref[q], cot)
    value_n = -2.0 * (cot / (numer + EPS))
    value_d = 2.0 * (cot * total_tx / (denom + EPS))
    scale_n = jnp.zeros_like(square)
    scale_d = jnp.zeros_like(square)
    for q in range(patches):
        inside = ids == q
        scale_n = jnp.where(inside, value_n[q : q + 1, :], scale_n)
        scale_d = jnp.where(inside, value_d[q : q + 1, :], scale_d)
    return scale_n, scale_d


def gradient_kernel(
    total_tx,
    cot_ref,
    here_ref,
    there_ref,
    ids_ref,
    slope_sum_ref,
    tx_path_ref,
    slope_ref,
    path_ref,
    out_ref,
    all_ref,
    bg_ref,
    bg_lane_ref,
    grad_ref,
):
    rows, cells, _ = path_ref.shape
    pairs = here_ref.shape[1]
    blocks = 2 * pairs
    count = slope_sum_ref.shape[0]
    per = 128 // blocks
    together = grad_ref.shape[0]
    core = lax.axis_index("c")
    me = (lax.axis_index("x") * lax.axis_size("zl") + lax.axis_index("zl")) * 2 + core

    for row in range(count + 2):
        here = here_ref[row]
        there = there_ref[row]
        all_ref[row, pl.ds(0, pairs, stride=2), :] = jnp.where(core == 0, here, there)
        all_ref[row, pl.ds(1, pairs, stride=2), :] = jnp.where(core == 0, there, here)
    coherent = all_ref[count]
    power = all_ref[count + 1]
    scale_n, scale_d = patch_scales(total_tx, cot_ref, ids_ref[...] // PP, coherent, power)
    common = coherent * scale_n
    for t in range(count):
        bg_ref[t] = common + all_ref[t] * scale_d
    for half in range(count // per):
        stack = [bg_ref[half * per + i] for i in range(per)]
        bg_lane_ref[:, half * 128 : (half + 1) * 128] = jnp.concatenate(stack, axis=0).T
    start = jnp.zeros((cells, PB), F32)
    for t in range(count):
        own = bg_ref[t, pl.ds(me, 1), :] * slope_sum_ref[t : t + 1, :]
        start = start + tx_path_ref[t].astype(F32) * own

    def receivers(step, acc):
        acc = list(acc)
        for i in range(together):
            r = step * together + i
            grad = None
            for half in range(count // per):
                lanes = slice(half * 128, (half + 1) * 128)
                term = slope_ref[r, :, lanes] * bg_lane_ref[:, lanes]
                grad = term if grad is None else grad + term
            grad = grad.T
            total = grad[0:blocks]
            for group in range(1, per):
                total = total + grad[group * blocks : (group + 1) * blocks]
            grad_ref[i] = total
            for k in range(blocks):
                paths = path_ref[r, :, k * PB : (k + 1) * PB].astype(F32)
                acc[k % 2] = acc[k % 2] + paths * grad_ref[i, k : k + 1, :]
        return tuple(acc)

    acc = lax.fori_loop(0, rows // together, receivers, (start, jnp.zeros_like(start)))
    row = jnp.sum((acc[0] + acc[1]).T, axis=0, keepdims=True) * LN2
    row = jnp.concatenate([row] * (PB // cells), axis=1)
    out_ref[...] = jnp.broadcast_to(row, out_ref.shape)


def groups_along(axes, order):
    sizes = [size for _, size in FINE]
    ids = np.arange(math.prod(sizes)).reshape(sizes)
    moved = [EVERY.index(axis) for axis in axes]
    ids = np.moveaxis(ids, moved, range(-len(moved), 0)).reshape(-1, len(order))
    return ids[:, list(order)].tolist()


def exchange(array, axes, order):
    return lax.all_to_all(array, EVERY, 0, 0, axis_index_groups=groups_along(axes, order))


def params(megabytes):
    return pltpu.CompilerParams(vmem_limit_bytes=megabytes * 1024 * 1024)


def whole(shape):
    return pl.BlockSpec(shape, lambda *_: (0,) * len(shape))


def shaped(*shape):
    return jax.ShapeDtypeStruct(shape, F32)


def in_hbm(array):
    return pltpu.with_memory_space_constraint(array, pltpu.HBM)


def tx_delays(s_row, tx_paths, rx_size):
    tx_count, _, own_pixels = tx_paths.shape
    return pl.pallas_call(
        tx_delay_kernel,
        in_specs=[pl.BlockSpec(memory_space=pl.ANY)] * 2,
        out_shape=shaped(rx_size, tx_count, own_pixels),
        scratch_shapes=[
            pltpu.VMEM(s_row.shape, s_row.dtype),
            pltpu.VMEM(tx_paths.shape, tx_paths.dtype),
            pltpu.SemaphoreType.DMA((2,)),
        ],
        compiler_params=params(4),
        name="tx_delay",
    )(in_hbm(s_row), in_hbm(tx_paths))


def prepare(s_row, rx_paths, traces, tap_start):
    rx_count, cells, pixels = rx_paths.shape
    tx_count, _, samples = traces.shape
    blocks = pixels // PB
    rows = 8
    vmem = pl.BlockSpec(memory_space=pltpu.VMEM)
    arrays = (s_row, rx_paths, traces, tap_start)
    return pl.pallas_call(
        prepare_kernel,
        in_specs=[pl.BlockSpec(memory_space=pl.ANY)] * len(arrays),
        out_specs=[vmem] * 2,
        out_shape=[shaped(rx_count, PB, 128), shaped(rx_count, W, tx_count * blocks)],
        scratch_shapes=[pltpu.VMEM(array.shape, array.dtype) for array in arrays]
        + [
            pltpu.VMEM((tx_count, rx_count, samples), F32),
            pltpu.VMEM((rows, blocks, PB), F32),
            pltpu.SemaphoreType.DMA((len(arrays) - 1 + rx_count // rows,)),
        ],
        compiler_params=params(20),
        name="prepare",
    )(*(in_hbm(array) for array in arrays))


def focus(tx_delay, rx_delay, window, rx_paths):
    blocks, tx_count, _ = tx_delay.shape
    rx_count = rx_delay.shape[0]
    lanes = tx_count * blocks
    vmem = pl.BlockSpec(memory_space=pltpu.VMEM)
    return pl.pallas_call(
        focus_kernel,
        in_specs=[vmem, vmem, vmem, pl.BlockSpec(memory_space=pl.ANY)],
        out_specs=[vmem] * 4,
        out_shape=[
            shaped(rx_count, PB, lanes),
            shaped(blocks // 2, 2 * tx_count, PB),
            shaped(blocks // 2, 2 * tx_count, PB),
            jax.ShapeDtypeStruct(rx_paths.shape, rx_paths.dtype),
        ],
        scratch_shapes=[pltpu.VMEM((PB, lanes), F32)] * 3
        + [pltpu.VMEM((128, PB), F32), pltpu.SemaphoreType.DMA],
        compiler_params=params(20),
        name="focus",
    )(tx_delay, rx_delay, window, in_hbm(rx_paths))


def gradient(total_tx, parts, patch_cotangent, here, there, pixel_order, slope_sum, tx_paths, slope, rx_paths):
    rx_count = rx_paths.shape[0]
    blocks = 2 * here.shape[1]
    tx_count = tx_paths.shape[0]
    lanes = tx_count * blocks
    together = 8
    vmem = pl.BlockSpec(memory_space=pltpu.VMEM)
    return pl.pallas_call(
        lambda *refs: gradient_kernel(total_tx, *refs),
        in_specs=[pl.BlockSpec(memory_space=pltpu.SMEM)] + [vmem] * 7,
        out_specs=vmem,
        out_shape=shaped(parts, PB),
        scratch_shapes=[
            pltpu.VMEM((tx_count + 2, blocks, PB), F32),
            pltpu.VMEM((tx_count, blocks, PB), F32),
            pltpu.VMEM((PB, lanes), F32),
            pltpu.VMEM((together, blocks, PB), F32),
        ],
        compiler_params=params(20),
        name="gradient",
    )(
        patch_cotangent,
        here,
        there,
        pixel_order.reshape(blocks, PB),
        slope_sum,
        tx_paths,
        slope,
        rx_paths,
    )


def local(kernel, name, out_shape, *arrays):
    return pl.pallas_call(
        kernel, out_shape=out_shape, compiler_params=params(4), name=name
    )(*arrays)


def on_device(slowness, tx_paths, rx_paths, traces, tap_start, pixel_order, patch_cotangent):
    tx_count, cells, _ = tx_paths.shape
    rx_size = lax.axis_size(RX)
    tx_size = lax.axis_size(TX)
    x_size = lax.axis_size("x")
    near = lax.axis_size("zl")
    pairs = x_size * near
    s_row = slowness.reshape(1, cells)
    swap = [(0, 1), (1, 0)]

    delay = tx_delays(s_row, tx_paths, rx_size)
    rx_delay, window = prepare(s_row, rx_paths, traces, tap_start)
    tx_delay = lax.all_to_all(delay, RX, 0, 0)
    slope, keep, give, path_copy = focus(tx_delay, rx_delay, window, rx_paths)
    got = lax.ppermute(give, "c", swap)
    part = local(pair_sum_kernel, "sum_cores", shaped(*keep.shape), keep, got)
    part = exchange(part.reshape(x_size, near, 2 * tx_count, PB), ("x",), X_ORDER)
    rows = (near + 1) * tx_count
    part = local(sum_x_kernel, "sum_x", shaped(2 * near, rows, PB), part)
    part = exchange(part, ("zh", "zl"), Z_ORDER)
    rows = near * (tx_count + 2)
    part, slope_sum = local(
        sum_z_kernel,
        "sum_z",
        [shaped(x_size * lax.axis_size("y"), rows, PB), shaped(tx_count, PB)],
        part,
    )
    part = lax.all_to_all(part, ("x", "y"), 0, 0)
    here = local(sum_y_kernel, "sum_y", shaped(tx_count + 2, pairs, PB), part)
    there = lax.ppermute(here, "c", swap)
    share = gradient(
        tx_count * tx_size,
        tx_size * rx_size,
        patch_cotangent,
        here,
        there,
        pixel_order,
        slope_sum,
        tx_paths,
        slope,
        path_copy,
    )
    share = lax.all_to_all(share, TX + RX, 0, 0, tiled=True)
    return local(total_kernel, "total", shaped(cells), share)


def solution(mesh):
    fine = Mesh(mesh.devices.reshape([size for _, size in FINE]), EVERY)
    in_specs = (
        P(),
        P(TX, None, RX),
        P(RX, None, None),
        P(TX, RX, None),
        P(TX, RX, None),
        P(),
        P(),
    )
    out_specs = P()
    return jax.shard_map(
        on_device, mesh=fine, in_specs=in_specs, out_specs=out_specs, check_vma=False
    )
```
